128 devices in a mesh: ctx: 32 (over y_lo, z, x), tp: 4 (over y_hi, core).
Axes of the slice: x: 4, y: 4 (y_hi: 2, y_lo: 2; y = y_hi * 2 + y_lo), z: 4, core: 2. Of those that a mesh axis runs over, the one named last changes fastest.
Arguments:
- signal: bfloat16 [256, 65536], P('tp', 'ctx'), may hold values from -6 to 6
- grad_out: bfloat16 [256, 65536], P('tp', 'ctx'), may hold values from -6 to 6
- long_filter: float32 [65536], P('ctx'), may hold values from -2 to 2, as said below
- short_filter: float32 [128], replicated, may hold values from -0.5 to 0.5
- long_skip: float32 [256], P('tp'), may hold values from 0.5 to 1.5
- short_skip: float32 [256], P('tp'), may hold values from 0.25 to 1.25
Outputs:
- signal_grad: bfloat16 [256, 65536], P('tp', 'ctx')
- long_grad: float32 [65536], P(('ctx', 'tp'))
- short_grad: float32 [128], replicated
The draws below stay inside these ranges and needn't reach their ends.
Inputs may be any that keep to these rules, and one draw needn't show every extreme that they name: `long_filter`: one filter shared by all channels of the group.
All inputs are finite; a program needn't handle non-finite values.
Results may differ from the reference program's by a relative error of at most 0.00045.
Values may be sent and summed in bfloat16 or wider, within the bound.
A program may use at most 64 MiB of HBM per device.

```python
import math
import jax
import jax.numpy as jnp
from jax import lax

CHANNELS = 256
TAPS = 128
LENGTH = 65536


def draw_long_filter(key, part):
    key = jax.random.fold_in(key, 7)
    key_noise, key_rate, key_span = jax.random.split(key, 3)
    positions = jnp.arange(LENGTH, dtype=jnp.float32)
    noise_vals = jax.random.normal(key_noise, (LENGTH,), jnp.float32)
    decay_rate = jax.random.uniform(key_rate, (), jnp.float32, 0.5, 2.0)
    fast_span = jax.random.uniform(key_span, (), jnp.float32, 30.0, 50.0)
    fast_part = jnp.exp(-positions / fast_span) * jnp.sqrt(1.0 / fast_span)
    slow_part = jnp.exp(-decay_rate * positions / LENGTH) * jnp.sqrt(decay_rate / LENGTH)
    return jnp.clip(noise_vals * (fast_part + slow_part), -2.0, 2.0)


def level_of(own_key, extent, pieces, least, high):
    gain, own = 1.0, jax.random.fold_in(own_key, 6)
    for axis_at, blocks in pieces:
        draws = jnp.exp(jax.random.uniform(jax.random.fold_in(own, axis_at), (blocks,), jnp.float32, least / len(pieces), high / len(pieces)))
        gain = gain * jnp.repeat(draws, extent[axis_at] // blocks).reshape([-1 if axis == axis_at else 1 for axis in range(len(extent))])
    return gain


def normal_values(stream_key, dims, scale, reach, cuts=(), held_as=jnp.bfloat16):
    array = jax.random.normal(stream_key, dims, jnp.float32) * scale
    if len(cuts) > 0:
        array = level_of(stream_key, dims, cuts, -0.22, 0.18) * array
    return jnp.clip(array, min=-reach, max=reach).astype(held_as)


def setup_inputs(seed: int = 0) -> dict:
    seeds = jax.random.split(jax.random.key(seed), 7)
    signal = normal_values(seeds[0], (CHANNELS, LENGTH), 1.0, 6.0, ((0, 4), (1, 32)))
    grad_out = normal_values(seeds[1], (CHANNELS, LENGTH), 1.0, 6.0, ((0, 4), (1, 32)))
    long_filter = draw_long_filter(jax.random.fold_in(seeds[6], 71), 0)
    short_filter = normal_values(seeds[3], (TAPS,), TAPS ** -0.5, 0.5, (), jnp.float32)
    long_skip = jnp.clip(0.5 + 1.0 * jax.random.uniform(seeds[4], (CHANNELS,), jnp.float32) ** level_of(seeds[4], (CHANNELS,), ((0, 4),), -0.2, 0.2), 0.5, 1.5)
    short_skip = jnp.clip(0.25 + 1.0 * jax.random.uniform(seeds[5], (CHANNELS,), jnp.float32) ** level_of(seeds[5], (CHANNELS,), ((0, 4),), -0.2, 0.2), 0.25, 1.25)
    return {"signal": signal, "grad_out": grad_out, "long_filter": long_filter, "short_filter": short_filter, "long_skip": long_skip, "short_skip": short_skip}


def reference(signal, grad_out, long_filter, short_filter, long_skip, short_skip):
    channels_all, seq_len = signal.shape
    padded_len = 2 * seq_len
    taps_len = short_filter.shape[0]
    group_len = math.gcd(channels_all, 32)
    group_count = channels_all // group_len
    filter_spec = jnp.fft.rfft(long_filter.astype(jnp.float32), n=padded_len)
    short_spec = jnp.fft.rfft(short_filter.astype(jnp.float32), n=padded_len)

    def per_group(carry, inputs):
        long_acc, short_acc = carry
        sig_block, cot_block, long_gain, short_gain = inputs
        sig_block = sig_block.astype(jnp.float32)
        cot_block = cot_block.astype(jnp.float32)
        sig_spec = jnp.fft.rfft(sig_block, n=padded_len)
        hidden = jnp.fft.irfft(sig_spec * filter_spec[None, :], n=padded_len)[:, :seq_len] + long_gain[:, None] * sig_block
        cot_spec = jnp.fft.rfft(cot_block, n=padded_len)
        back_short = jnp.fft.irfft(cot_spec * jnp.conj(short_spec)[None, :], n=padded_len)[:, :seq_len] + short_gain[:, None] * cot_block
        hidden_spec = jnp.fft.rfft(hidden, n=padded_len)
        short_term = jnp.sum(jnp.fft.irfft(cot_spec * jnp.conj(hidden_spec), n=padded_len)[:, :taps_len], axis=0)
        back_spec = jnp.fft.rfft(back_short, n=padded_len)
        sig_grad = jnp.fft.irfft(back_spec * jnp.conj(filter_spec)[None, :], n=padded_len)[:, :seq_len] + long_gain[:, None] * back_short
        long_term = jnp.sum(jnp.fft.irfft(back_spec * jnp.conj(sig_spec), n=padded_len)[:, :seq_len], axis=0)
        return (long_acc + long_term, short_acc + short_term), sig_grad.astype(jnp.bfloat16)

    inputs = (signal.reshape(group_count, group_len, seq_len),
              grad_out.reshape(group_count, group_len, seq_len),
              long_skip.astype(jnp.float32).reshape(group_count, group_len),
              short_skip.astype(jnp.float32).reshape(group_count, group_len))
    init = (jnp.zeros((seq_len,), jnp.float32), jnp.zeros((taps_len,), jnp.float32))
    (long_grad, short_grad), grads = lax.scan(per_group, init, inputs)
    return grads.reshape(channels_all, seq_len), long_grad, short_grad
```

```python
import math

import jax
import jax.numpy as jnp
import ml_dtypes
import numpy as np
from jax import lax
from jax.experimental import pallas as pl
from jax.experimental.pallas import tpu as pltpu
from jax.sharding import PartitionSpec as P

MESH = pl.DeviceIdType.MESH
F32, BF16 = jnp.float32, jnp.bfloat16
N1, N2 = 512, 128
LEN = N1 * N2


def split_np(x):
    x = x.astype(np.float32)
    hi = x.astype(ml_dtypes.bfloat16)
    lo = (x - hi.astype(np.float32)).astype(ml_dtypes.bfloat16)
    return hi, lo


def tables():
    k = np.arange(N1, dtype=np.float64)[:, None] + 0.25
    n = np.arange(N1, dtype=np.float64)[None, :]
    ang = -2 * np.pi * np.mod(k * n, N1) / N1
    fwd = np.concatenate([np.cos(ang), np.sin(ang)], axis=0)
    f_hi, f_lo = split_np(fwd)
    f_cat = np.concatenate([f_hi, f_lo], axis=1)
    i_hi, i_lo = np.ascontiguousarray(f_hi.T), np.ascontiguousarray(f_lo.T)
    i_cat = np.concatenate([i_hi, i_lo], axis=1)
    m = np.arange(N2, dtype=np.float64)
    ang = -2 * np.pi * k * m[None, :] / LEN
    twist = np.concatenate([np.cos(ang), np.sin(ang)], axis=1).astype(np.float32)
    ang = -2 * np.pi * np.mod(m[:, None] * m[None, :], N2) / N2
    br, bi = np.cos(ang), np.sin(ang)
    b_hi, b_lo = split_np(np.block([[br, bi], [-bi, br]]))
    b_cat = np.concatenate([b_hi, b_hi, b_lo], axis=0)
    c_hi, c_lo = split_np(np.block([[br, -bi], [bi, br]]) / LEN)
    c_cat = np.concatenate([c_hi, c_hi, c_lo], axis=0)
    return f_cat, i_cat, twist, b_cat, c_cat


def dot(a, b):
    return jnp.dot(a, b, preferred_element_type=F32)


def split(x):
    hi = x.astype(BF16)
    return hi, (x - hi.astype(F32)).astype(BF16)


def split3(x):
    hi, lo = split(x)
    return jnp.concatenate([hi, lo, hi], axis=1)


def rows_of(i, size):
    return pl.ds(pl.multiple_of(i * size, size), size)


def twist_and_mix(yr, yi, tw, b_cat):
    tr, ti = tw[:, :N2], tw[:, N2:]
    y = jnp.concatenate([yr * tr - yi * ti, yi * tr + yr * ti], axis=1)
    return dot(split3(y), b_cat)


def forward_exact(x, f_cat, twist, b_cat, z_refs, block=128):
    x2 = jnp.concatenate([x, x], axis=0)

    def step(i, carry):
        r = rows_of(i, block)
        yr = dot(f_cat[r, :], x2)
        yi = dot(f_cat[pl.ds(pl.multiple_of(N1 + i * block, block), block), :], x2)
        tw = twist[r, :]
        for q, z in enumerate(z_refs):
            s = slice(q * N2, (q + 1) * N2)
            z[r, :] = twist_and_mix(yr[:, s], yi[:, s], tw, b_cat[...])
        return carry

    lax.fori_loop(0, N1 // block, step, 0)


def forward_split(hi, lo, f_cat, twist, b_cat, z_refs, block=128):
    x2 = jnp.concatenate([hi, hi], axis=0)

    def step(i, carry):
        r = rows_of(i, block)
        ri = pl.ds(pl.multiple_of(N1 + i * block, block), block)
        yr = dot(f_cat[r, :], x2) + dot(f_cat[r, :N1], lo)
        yi = dot(f_cat[ri, :], x2) + dot(f_cat[ri, :N1], lo)
        tw = twist[r, :]
        for q, z in enumerate(z_refs):
            s = slice(q * N2, (q + 1) * N2)
            z[r, :] = twist_and_mix(yr[:, s], yi[:, s], tw, b_cat[...])
        return carry

    lax.fori_loop(0, N1 // block, step, 0)


def inverse_pair(left, right, i_cat, twist, c_cat, y_hi, y_lo, out, block=128):
    def step(i, carry):
        r = rows_of(i, block)
        ri = pl.ds(pl.multiple_of(N1 + i * block, block), block)
        tr, ti = twist[r, :N2], twist[r, N2:]
        for c in range(2):
            ar, ai = left[c][r, :N2], left[c][r, N2:]
            br, bi = right[c][r, :N2], right[c][r, N2:]
            z = jnp.concatenate([ar * br + ai * bi, ai * br - ar * bi], axis=1)
            y = dot(split3(z), c_cat[...])
            yr, yi = y[:, :N2], y[:, N2:]
            s = slice(c * N2, (c + 1) * N2)
            y_hi[r, s], y_lo[r, s] = split(yr * tr + yi * ti)
            y_hi[ri, s], y_lo[ri, s] = split(yi * tr - yr * ti)
        return carry

    lax.fori_loop(0, N1 // block, step, 0)
    hi2 = jnp.concatenate([y_hi[...], y_hi[...]], axis=0)

    def final(i, carry):
        r = rows_of(i, block)
        out[r, :] = dot(i_cat[r, :], hi2) + dot(i_cat[r, : 2 * N1], y_lo[...])
        return carry

    lax.fori_loop(0, N1 // block, final, 0)


def dot3(a, b):
    ah, al = split(a)
    bh, bl = split(b)
    return dot(ah, bh) + (dot(ah, bl) + dot(al, bh))


def dot3_nt(a, b):
    def nt(x, y):
        return lax.dot_general(x, y, (((1,), (1,)), ((), ())), preferred_element_type=F32)

    ah, al = split(a)
    bh, bl = split(b)
    return nt(ah, bh) + (nt(ah, bl) + nt(al, bh))


def swap_matrix():
    i = lax.broadcasted_iota(jnp.int32, (256, 256), 0)
    j = lax.broadcasted_iota(jnp.int32, (256, 256), 1)
    same = (i // 16 == j % 16) & (i % 16 == j // 16)
    return jnp.where(same, 1.0, 0.0).astype(BF16)


def long_and_short(r_buf, corr, f_buf, w_row, alpha, lam):
    r0, r1 = corr[:, :N2], corr[:, N2:]
    r_sum = r0 + r1
    r_buf[:N1, :] = r_sum
    r_pair = jnp.concatenate([r_sum, r_buf[pl.ds(1, N1), :]], axis=1)
    zero = jnp.zeros((1, N2), F32)
    base = jnp.broadcast_to(jnp.concatenate([w_row, zero], axis=1), (N2, 2 * N2))
    toep = pltpu.roll(base, 0, 1, stride=1, stride_axis=0)
    long = dot3_nt(r_pair, toep) + (alpha[0] * r0 + alpha[1] * r1)
    cross = dot3(jnp.transpose(f_buf[8 : 8 + N1, :]), r_pair)
    i = lax.broadcasted_iota(jnp.int32, (N2, N2), 0)
    j = lax.broadcasted_iota(jnp.int32, (N2, N2), 1)
    flip = jnp.where(i + j == N2 - 1, 1.0, 0.0).astype(BF16)
    ch, cl = split(cross)
    back = dot(flip, ch) + dot(flip, cl)
    diag = pltpu.roll(back, N2 + 1, 1, stride=1, stride_axis=0)
    short = jnp.sum(diag, axis=0, keepdims=True)[:, :N2]
    return long, short + (lam[0] * r0[:1, :] + lam[1] * r1[:1, :])


def filters(f_buf, w_row, alpha, lam, v_hi, v_lo):
    f = f_buf[8 : 8 + N1, :]
    f_pair = jnp.concatenate([f_buf[pl.ds(7, N1), :], f], axis=1)
    zero = jnp.zeros((1, N2), F32)
    base = jnp.broadcast_to(jnp.concatenate([zero, w_row], axis=1), (2 * N2, 2 * N2))
    toep = pltpu.roll(base, 0, 1, stride=1, stride_axis=0)[:, :N2]
    u = dot3(f_pair, toep)
    first_row = lax.broadcasted_iota(jnp.int32, (8, N2), 0) == 0
    first = first_row & (lax.broadcasted_iota(jnp.int32, (8, N2), 1) == 0)
    for c in range(2):
        s = slice(c * N2, (c + 1) * N2)
        v = u + alpha[c] * f
        extra = jnp.where(first_row, lam[c] * w_row, 0.0) + jnp.where(first, lam[c] * alpha[c], 0.0)
        v = jnp.concatenate([v[:8] + extra, v[8:]], axis=0)
        v_hi[:, s], v_lo[:, s] = split(v)


def kernel(
    n_ctx, n_tp,
    sig, cot, filt, w_in, lam_in, alpha_in, f_tab, i_tab, t_tab, b_tab, c_tab,
    sg_out, long_out, short_out,
    sig_v, cot_v, filt_v, f_cat, i_cat, twist, b_cat, c_cat,
    send, recv, f_buf, zs0, zg0, zs1, zg1, y_hi, y_lo, corr, r_buf,
    l_send, l_recv, t_send, t_recv, v_hi, v_lo, zv0, zv1, sg_send, sg_recv,
    load_sem, tab_sem, send_sem, recv_sem,
):
    me, tp = lax.axis_index("ctx"), lax.axis_index("tp")

    def peer(i):
        return lax.rem(me + i, n_ctx)

    def tp_peer(i):
        return lax.rem(tp + i, n_tp)

    barrier = pltpu.get_barrier_semaphore()

    def greet(i, carry):
        pl.semaphore_signal(barrier, inc=1, device_id={"ctx": peer(i)}, device_id_type=MESH)
        return carry

    def greet_tp(i, carry):
        pl.semaphore_signal(barrier, inc=1, device_id={"tp": tp_peer(i)}, device_id_type=MESH)
        return carry

    loads = [
        pltpu.make_async_copy(src, dst, load_sem.at[i])
        for i, (src, dst) in enumerate([(sig, sig_v), (cot, cot_v), (filt, filt_v)])
    ]
    for c in loads:
        c.start()
    lax.fori_loop(1, n_ctx, greet, 0)
    lax.fori_loop(1, n_tp, greet_tp, 0)
    tabs = [
        pltpu.make_async_copy(src, dst, tab_sem.at[i])
        for i, (src, dst) in enumerate(
            [(f_tab, f_cat), (t_tab, twist), (b_tab, b_cat), (c_tab, c_cat), (i_tab, i_cat)]
        )
    ]
    for c in tabs:
        c.start()
    f_buf[:8, :] = jnp.zeros((8, N2), F32)
    r_buf[N1:, :] = jnp.zeros((8, N2), F32)
    swap = swap_matrix()
    for c in loads:
        c.wait()
    for g in range(4):
        ch = slice(16 * g, 16 * (g + 1))
        x = jnp.concatenate(
            [
                jnp.concatenate([v[ch, N2 * a : N2 * (a + 1)] for a in range(16)], axis=0)
                for v in (sig_v, cot_v)
            ],
            axis=1,
        )
        y = dot(swap, x).astype(BF16)
        send[ch, 0] = y[:, :N2].reshape(16, 16, N2)
        send[ch, 1] = y[:, N2:].reshape(16, 16, N2)
    pl.semaphore_wait(barrier, n_ctx + n_tp - 2)

    rows_me = pl.ds(pl.multiple_of(16 * me, 16), 16)

    def remote(src, dst, k, where):
        return pltpu.make_async_remote_copy(
            src_ref=src, dst_ref=dst, send_sem=send_sem.at[k], recv_sem=recv_sem.at[k],
            device_id=where, device_id_type=MESH,
        )

    def finish(ref, sem):
        pltpu.make_async_copy(ref, ref, sem).wait()

    def send_in(i, carry):
        e = peer(i)
        remote(send.at[pl.ds(2 * e, 2)], recv.at[:, :, rows_me, :], 0, {"ctx": e}).start()
        return carry

    def send_filter(i, carry):
        e = peer(i)
        remote(filt_v, f_buf.at[pl.ds(pl.multiple_of(8 + 16 * me, 8), 16), :], 1, {"ctx": e}).start()
        return carry

    pltpu.make_async_copy(send.at[pl.ds(2 * me, 2)], recv.at[:, :, rows_me, :], recv_sem.at[0]).start()
    pltpu.make_async_copy(
        filt_v, f_buf.at[pl.ds(pl.multiple_of(8 + 16 * me, 8), 16), :], recv_sem.at[1]
    ).start()
    lax.fori_loop(1, n_ctx, send_in, 0)
    lax.fori_loop(1, n_ctx, send_filter, 0)

    w_row = w_in[...]
    alpha = (alpha_in[2 * me], alpha_in[2 * me + 1])
    lam = (lam_in[2 * me], lam_in[2 * me + 1])
    for c in tabs:
        c.wait()

    finish(recv, recv_sem.at[0])
    x = jnp.concatenate([recv[0, 0], recv[0, 1], recv[1, 0], recv[1, 1]], axis=1)
    forward_exact(x, f_cat, twist, b_cat, (zs0, zg0, zs1, zg1))
    inverse_pair((zg0, zg1), (zs0, zs1), i_cat, twist, c_cat, y_hi, y_lo, corr)

    finish(f_buf.at[pl.ds(8, N1), :], recv_sem.at[1])
    long, short = long_and_short(r_buf, corr, f_buf, w_row, alpha, lam)
    l_send[:, :16, :] = long.reshape(32, 16, N2)
    l_send[:, 16:, :] = jnp.broadcast_to(short.reshape(1, 1, N2), (32, 8, N2))

    def send_long(i, carry):
        e = peer(i)
        remote(l_send.at[e], l_recv.at[me], 2, {"ctx": e}).start()
        return carry

    pltpu.make_async_copy(l_send.at[me], l_recv.at[me], recv_sem.at[2]).start()
    lax.fori_loop(1, n_ctx, send_long, 0)

    filters(f_buf, w_row, alpha, lam, v_hi, v_lo)
    forward_split(v_hi[...], v_lo[...], f_cat, twist, b_cat, (zv0, zv1))
    inverse_pair((zg0, zg1), (zv0, zv1), i_cat, twist, c_cat, y_hi, y_lo, corr)
    sg_send[0] = corr[:, :N2].astype(BF16)
    sg_send[1] = corr[:, N2:].astype(BF16)

    def send_back(i, carry):
        e = peer(i)
        rows = pl.ds(pl.multiple_of(16 * e, 16), 16)
        remote(sg_send.at[:, rows, :], sg_recv.at[pl.ds(2 * me, 2)], 4, {"ctx": e}).start()
        return carry

    pltpu.make_async_copy(
        sg_send.at[:, rows_me, :], sg_recv.at[pl.ds(2 * me, 2)], recv_sem.at[4]
    ).start()
    lax.fori_loop(1, n_ctx, send_back, 0)

    finish(l_recv, recv_sem.at[2])
    total = l_recv[0]
    for d in range(1, 32):
        total = total + l_recv[d]
    for t in range(4):
        t_send[t, :4, :] = total[4 * t : 4 * (t + 1)]
        t_send[t, 4:, :] = total[16:20]

    def send_tp(i, carry):
        t = tp_peer(i)
        remote(t_send.at[t], t_recv.at[tp], 3, {"tp": t}).start()
        return carry

    pltpu.make_async_copy(t_send.at[tp], t_recv.at[tp], recv_sem.at[3]).start()
    lax.fori_loop(1, n_tp, send_tp, 0)

    finish(sg_recv, recv_sem.at[4])
    for g in range(2):
        x = jnp.concatenate(
            [sg_recv[32 * g + 16 * h : 32 * g + 16 * (h + 1)].reshape(256, N2) for h in range(2)], axis=1
        )
        y = dot(swap, x).astype(BF16)
        for h in range(2):
            ch = slice(32 * g + 16 * h, 32 * g + 16 * (h + 1))
            for a in range(16):
                sg_out[ch, N2 * a : N2 * (a + 1)] = y[16 * a : 16 * (a + 1), h * N2 : (h + 1) * N2]
    finish(t_recv, recv_sem.at[3])
    whole = (t_recv[0] + t_recv[1]) + (t_recv[2] + t_recv[3])
    long_out[...] = whole[:4]
    short_out[...] = whole[4:5]
    finish(send.at[pl.ds(0, 62)], send_sem.at[0])
    finish(f_buf.at[pl.ds(8, 16 * 31), :], send_sem.at[1])
    finish(l_send.at[pl.ds(0, 31)], send_sem.at[2])
    finish(t_send.at[pl.ds(0, 3)], send_sem.at[3])
    finish(sg_recv.at[pl.ds(0, 62)], send_sem.at[4])


def shards(signal, grad_out, long_filter, short_filter, long_skip, short_skip):
    n_ctx, n_tp = lax.axis_size("ctx"), lax.axis_size("tp")
    consts = [jnp.asarray(t) for t in tables()]
    any_spec = pl.BlockSpec(memory_space=pl.ANY)
    vmem = pl.BlockSpec(memory_space=pltpu.VMEM)
    smem = pl.BlockSpec(memory_space=pltpu.SMEM)
    V = pltpu.VMEM
    spec = V((N1, 2 * N2), F32)
    sg, long, short = pl.pallas_call(
        lambda *refs: kernel(n_ctx, n_tp, *refs),
        out_shape=(
            jax.ShapeDtypeStruct((64, 2048), BF16),
            jax.ShapeDtypeStruct((4, N2), F32),
            jax.ShapeDtypeStruct((1, N2), F32),
        ),
        in_specs=[any_spec] * 3 + [vmem, smem, smem] + [any_spec] * 5,
        out_specs=(vmem, vmem, vmem),
        scratch_shapes=[
            V((64, 2048), BF16), V((64, 2048), BF16), V((16, N2), F32),
            V((1024, 1024), BF16), V((512, 2048), BF16), V((N1, 2 * N2), F32),
            V((768, 256), BF16), V((768, 256), BF16),
            V((64, 2, 16, N2), BF16), V((2, 2, N1, N2), BF16), V((N1 + 8, N2), F32),
            spec, spec, spec, spec,
            V((2 * N1, 2 * N2), BF16), V((2 * N1, 2 * N2), BF16), spec, V((N1 + 8, N2), F32),
            V((32, 24, N2), F32), V((32, 24, N2), F32), V((4, 8, N2), F32), V((4, 8, N2), F32),
            V((N1, 2 * N2), BF16), V((N1, 2 * N2), BF16), spec, spec,
            V((2, N1, N2), BF16), V((64, 16, N2), BF16),
            pltpu.SemaphoreType.DMA((3,)), pltpu.SemaphoreType.DMA((5,)),
            pltpu.SemaphoreType.DMA((5,)), pltpu.SemaphoreType.DMA((5,)),
        ],
        compiler_params=pltpu.CompilerParams(
            collective_id=0, has_side_effects=True, vmem_limit_bytes=48 * 1024 * 1024
        ),
        cost_estimate=pl.CostEstimate(flops=6_000_000_000, bytes_accessed=8_000_000, transcendentals=0),
    )(
        signal, grad_out, long_filter.reshape(16, N2), short_filter.reshape(1, N2),
        long_skip, short_skip, *consts,
    )
    return sg, long.reshape(512), short.reshape(N2)


def solution(mesh):
    placed = (P("tp", "ctx"), P("tp", "ctx"), P("ctx"), P(), P("tp"), P("tp"))
    return jax.shard_map(
        shards,
        mesh=mesh,
        in_specs=placed,
        out_specs=(P("tp", "ctx"), P(("ctx", "tp")), P()),
        check_vma=False,
    )
```

```python
import math

import jax
import jax.numpy as jnp
import ml_dtypes
import numpy as np
from jax import lax
from jax.experimental import pallas as pl
from jax.experimental.pallas import tpu as pltpu
from jax.sharding import PartitionSpec as P

MESH = pl.DeviceIdType.MESH
F32, BF16 = jnp.float32, jnp.bfloat16
N1, N2 = 512, 128
LEN = N1 * N2
HALF = N1 // 2


def split_np(x):
    x = x.astype(np.float32)
    hi = x.astype(ml_dtypes.bfloat16)
    lo = (x - hi.astype(np.float32)).astype(ml_dtypes.bfloat16)
    return hi, lo


def tables():
    k = np.arange(N1, dtype=np.float64)[:, None] + 0.25
    kh = k[:HALF]
    fwd, inv = [], []
    for odd in range(2):
        n = 2 * np.arange(HALF, dtype=np.float64)[None, :] + odd
        ang = -2 * np.pi * np.mod(kh * n, N1) / N1
        hi, lo = split_np(np.concatenate([np.cos(ang), np.sin(ang)], axis=0))
        fwd.append(np.concatenate([hi, lo], axis=1))
        inv.append(np.concatenate([hi.T, lo.T], axis=1))
    m = np.arange(N2, dtype=np.float64)
    ang = -2 * np.pi * k * m[None, :] / LEN
    twist = np.concatenate([np.cos(ang), np.sin(ang)], axis=1).astype(np.float32)
    ang = -2 * np.pi * np.mod(m[:, None] * m[None, :], N2) / N2
    br, bi = np.cos(ang), np.sin(ang)
    b_hi, b_lo = split_np(np.block([[br, bi], [-bi, br]]))
    c_hi, c_lo = split_np(np.block([[br, -bi], [bi, br]]) / LEN)
    mix = np.concatenate([b_hi, b_hi, b_lo, c_hi, c_hi, c_lo])
    return np.concatenate(fwd), np.concatenate(inv), twist, mix


def dot(a, b):
    return jnp.dot(a, b, preferred_element_type=F32)


def split(x):
    hi = x.astype(BF16)
    return hi, (x - hi.astype(F32)).astype(BF16)


def split3(x):
    hi, lo = split(x)
    return jnp.concatenate([hi, lo, hi], axis=1)


def twice(x):
    return jnp.concatenate([x, x], axis=0)


def mix_forward(even, odd, twist, mix, z_refs):
    for q, z in enumerate(z_refs):
        s = slice(q * N2, (q + 1) * N2)
        er, ei, dr, di = even[:HALF, s], even[HALF:, s], odd[:HALF, s], odd[HALF:, s]
        for h, (xr, xi) in enumerate([(er + dr, ei + di), (er - dr, ei - di)]):
            r = slice(h * HALF, (h + 1) * HALF)
            tr, ti = twist[r, :N2], twist[r, N2:]
            y = jnp.concatenate([xr * tr - xi * ti, xi * tr + xr * ti], axis=1)
            z[r, :] = dot(split3(y), mix[:768, :])


def forward_exact(xe, xo, fwd, twist, mix, z_refs):
    mix_forward(dot(fwd[:N1, :], twice(xe)), dot(fwd[N1:, :], twice(xo)), twist, mix, z_refs)


def forward_split(xe, xo, fwd, twist, mix, z_refs):
    out = []
    for h, x in enumerate((xe, xo)):
        hi, lo = split(x)
        r = slice(h * N1, (h + 1) * N1)
        out.append(dot(fwd[r, :], twice(hi)) + dot(fwd[r, :HALF], lo))
    mix_forward(out[0], out[1], twist, mix, z_refs)


def inverse_pair(left, right, inv, twist, mix):
    plus, minus = [], []
    for a, b in zip(left, right):
        ys = []
        for h in range(2):
            r = slice(h * HALF, (h + 1) * HALF)
            ar, ai, br, bi = a[r, :N2], a[r, N2:], b[r, :N2], b[r, N2:]
            z = jnp.concatenate([ar * br + ai * bi, ai * br - ar * bi], axis=1)
            y = dot(split3(z), mix[768:, :])
            yr, yi = y[:, :N2], y[:, N2:]
            tr, ti = twist[r, :N2], twist[r, N2:]
            ys.append(jnp.concatenate([yr * tr + yi * ti, yi * tr - yr * ti], axis=0))
        plus.append(ys[0] + ys[1])
        minus.append(ys[0] - ys[1])
    out = []
    for h, y in enumerate((plus, minus)):
        hi, lo = split(jnp.concatenate(y, axis=1))
        r = slice(h * HALF, (h + 1) * HALF)
        out.append(dot(inv[r, :], twice(hi)) + dot(inv[r, :N1], lo))
    return out


def dot3(a, b):
    ah, al = split(a)
    bh, bl = split(b)
    return dot(ah, bh) + (dot(ah, bl) + dot(al, bh))


def dot3_nt(a, b):
    def nt(x, y):
        return lax.dot_general(x, y, (((1,), (1,)), ((), ())), preferred_element_type=F32)

    ah, al = split(a)
    bh, bl = split(b)
    return nt(ah, bh) + (nt(ah, bl) + nt(al, bh))


def one_hot(cond):
    return jnp.where(cond, 1.0, 0.0).astype(BF16)


def swap_matrix(back):
    i = lax.broadcasted_iota(jnp.int32, (256, 256), 0)
    j = lax.broadcasted_iota(jnp.int32, (256, 256), 1)
    if back:
        i, j = j, i
    p = i % 16
    return one_hot((i // 16 == j % 16) & (2 * (p % 8) + p // 8 == j // 16))


def long_and_short(r_buf, even, odd, f_buf, w_row, alpha, lam):
    re, ro = even[:, :N2] + even[:, N2:], odd[:, :N2] + odd[:, N2:]
    r_buf[:HALF, :] = re
    pair = jnp.concatenate(
        [jnp.concatenate([re, ro], axis=1), jnp.concatenate([ro, r_buf[pl.ds(1, HALF), :]], axis=1)], axis=0
    )
    zero = jnp.zeros((1, N2), F32)
    base = jnp.broadcast_to(jnp.concatenate([w_row, zero], axis=1), (N2, 2 * N2))
    toep = pltpu.roll(base, 0, 1, stride=1, stride_axis=0)
    long = dot3_nt(pair, toep)
    long_e = long[:HALF] + (alpha[0] * even[:, :N2] + alpha[1] * even[:, N2:])
    long_o = long[HALF:] + (alpha[0] * odd[:, :N2] + alpha[1] * odd[:, N2:])
    f = jnp.concatenate([f_buf[0, 8:, :], f_buf[1, 8:, :]], axis=0)
    cross = dot3(jnp.transpose(f), pair)
    i = lax.broadcasted_iota(jnp.int32, (N2, N2), 0)
    j = lax.broadcasted_iota(jnp.int32, (N2, N2), 1)
    flip = one_hot(i + j == N2 - 1)
    ch, cl = split(cross)
    diag = pltpu.roll(dot(flip, ch) + dot(flip, cl), N2 + 1, 1, stride=1, stride_axis=0)
    short = jnp.sum(diag, axis=0, keepdims=True)[:, :N2]
    return long_e, long_o, short + (lam[0] * even[:1, :N2] + lam[1] * even[:1, N2:])


def filters(f_buf, w_row, alpha, lam):
    fe, fo = f_buf[0, 8:, :], f_buf[1, 8:, :]
    pair = jnp.concatenate(
        [
            jnp.concatenate([f_buf[1, pl.ds(7, HALF), :], fe], axis=1),
            jnp.concatenate([fe, fo], axis=1),
        ],
        axis=0,
    )
    zero = jnp.zeros((1, N2), F32)
    base = jnp.broadcast_to(jnp.concatenate([zero, w_row], axis=1), (2 * N2, 2 * N2))
    toep = pltpu.roll(base, 0, 1, stride=1, stride_axis=0)[:, :N2]
    u = dot3(pair, toep)
    first_row = lax.broadcasted_iota(jnp.int32, (8, N2), 0) == 0
    first = first_row & (lax.broadcasted_iota(jnp.int32, (8, N2), 1) == 0)
    ve, vo = [], []
    for c in range(2):
        v = u[:HALF] + alpha[c] * fe
        extra = jnp.where(first_row, lam[c] * w_row, 0.0) + jnp.where(first, lam[c] * alpha[c], 0.0)
        ve.append(jnp.concatenate([v[:8] + extra, v[8:]], axis=0))
        vo.append(u[HALF:] + alpha[c] * fo)
    return jnp.concatenate(ve, axis=1), jnp.concatenate(vo, axis=1)


def halves(x):
    x = x.astype(F32).reshape(32, 16, N2)
    return x[:, :8].reshape(HALF, N2).astype(BF16), x[:, 8:].reshape(HALF, N2).astype(BF16)


def offsets():
    def far(o):
        return o[0] + min(o[1], 4 - o[1]) + min(o[2], 4 - o[2])

    out = [(y, z, x) for y in range(2) for z in range(4) for x in range(4)][1:]
    return sorted(out, key=lambda o: -far(o))


def kernel(
    n_ctx, n_tp,
    sig, cot, filt, w_in, lam_in, alpha_in, f_tab, i_tab, t_tab, m_tab,
    sg_recv, t_recv,
    sig_v, cot_v, filt_v, filt_s, w_v, lam_s, alpha_s, fwd, inv, twist, mix,
    send, recv, f_buf, zs0, zg0, zs1, zg1, zv0, zv1, r_buf, l_send, l_recv, t_send, sg_send,
    load_sem, send_sem, recv_sem,
):
    me, tp = lax.axis_index("ctx"), lax.axis_index("tp")
    my_y, my_z, my_x = me // 16, (me // 4) % 4, me % 4
    peers = [((my_y + y) % 2) * 16 + ((my_z + z) % 4) * 4 + (my_x + x) % 4 for y, z, x in offsets()]
    tp_peers = [(tp + i) % n_tp for i in (2, 3, 1)]
    n_peers = len(peers)

    barrier = pltpu.get_barrier_semaphore()
    loads = [
        pltpu.make_async_copy(src, dst, load_sem.at[i])
        for i, (src, dst) in enumerate(
            [(filt, filt_v), (sig, sig_v), (cot, cot_v), (w_in, w_v), (lam_in, lam_s), (alpha_in, alpha_s),
             (f_tab, fwd), (t_tab, twist), (m_tab, mix), (i_tab, inv)]
        )
    ]
    for c in loads:
        c.start()
    for e in peers:
        pl.semaphore_signal(barrier, inc=1, device_id={"ctx": e}, device_id_type=MESH)
    for t in tp_peers:
        pl.semaphore_signal(barrier, inc=1, device_id={"tp": t}, device_id_type=MESH)
    f_buf[:, :8, :] = jnp.zeros((2, 8, N2), F32)
    r_buf[HALF:, :] = jnp.zeros((8, N2), F32)
    swap = swap_matrix(False)
    for c in loads[:3]:
        c.wait()
    for h in range(2):
        for i in range(8):
            filt_s[h, i : i + 1, :] = filt_v[2 * i + h : 2 * i + h + 1, :]
    for g in range(4):
        ch = slice(16 * g, 16 * (g + 1))
        x = jnp.concatenate(
            [
                jnp.concatenate([v[ch, N2 * a : N2 * (a + 1)] for a in range(16)], axis=0)
                for v in (sig_v, cot_v)
            ],
            axis=1,
        )
        y = dot(swap, x).astype(BF16)
        send[ch, 0] = y[:, :N2].reshape(16, 16, N2)
        send[ch, 1] = y[:, N2:].reshape(16, 16, N2)
    pl.semaphore_wait(barrier, n_peers + len(tp_peers))

    rows_me = pl.ds(pl.multiple_of(16 * me, 16), 16)
    f_dst = f_buf.at[:, pl.ds(pl.multiple_of(8 + 8 * me, 8), 8), :]

    def remote(src, dst, k, where):
        pltpu.make_async_remote_copy(
            src_ref=src, dst_ref=dst, send_sem=send_sem.at[k], recv_sem=recv_sem.at[k],
            device_id=where, device_id_type=MESH,
        ).start()

    def local(src, dst, k):
        pltpu.make_async_copy(src, dst, recv_sem.at[k]).start()

    def finish(ref, sem):
        pltpu.make_async_copy(ref, ref, sem).wait()

    for e in peers:
        remote(filt_s, f_dst, 0, {"ctx": e})
    for c in range(2):
        for e in peers:
            remote(send.at[2 * e + c], recv.at[c, :, rows_me, :], 1 + c, {"ctx": e})
    local(filt_s, f_dst, 0)
    for c in range(2):
        local(send.at[2 * me + c], recv.at[c, :, rows_me, :], 1 + c)

    for c in loads[3:]:
        c.wait()
    w_row = w_v[...]
    alpha = (alpha_s[2 * me], alpha_s[2 * me + 1])
    lam = (lam_s[2 * me], lam_s[2 * me + 1])

    finish(f_buf.at[:, pl.ds(8, HALF), :], recv_sem.at[0])
    ve, vo = filters(f_buf, w_row, alpha, lam)
    forward_split(ve, vo, fwd, twist, mix, (zv0, zv1))
    for c, zs in enumerate(((zs0, zg0), (zs1, zg1))):
        finish(recv.at[c], recv_sem.at[1 + c])
        se, so = halves(recv[c, 0])
        ge, go = halves(recv[c, 1])
        forward_exact(
            jnp.concatenate([se, ge], axis=1), jnp.concatenate([so, go], axis=1), fwd, twist, mix, zs
        )
    even, odd = inverse_pair((zg0, zg1), (zs0, zs1), inv, twist, mix)
    long_e, long_o, short = long_and_short(r_buf, even, odd, f_buf, w_row, alpha, lam)
    l_send[:, :8, :] = long_e.reshape(32, 8, N2)
    l_send[:, 8:16, :] = long_o.reshape(32, 8, N2)
    l_send[:, 16:, :] = jnp.broadcast_to(short.reshape(1, 1, N2), (32, 8, N2))
    for e in peers:
        remote(l_send.at[e], l_recv.at[me], 3, {"ctx": e})
    local(l_send.at[me], l_recv.at[me], 3)

    even, odd = inverse_pair((zg0, zg1), (zv0, zv1), inv, twist, mix)
    for c in range(2):
        s = slice(c * N2, (c + 1) * N2)
        rows = jnp.concatenate([even[:, s].reshape(32, 8, N2), odd[:, s].reshape(32, 8, N2)], axis=1)
        sg_send[c] = rows.astype(BF16)
    sg_dst = sg_recv.at[pl.ds(2 * me, 2)]
    for e in peers:
        remote(sg_send.at[:, e], sg_dst, 4, {"ctx": e})
    local(sg_send.at[:, me], sg_dst, 4)

    finish(l_recv, recv_sem.at[3])
    total = l_recv[0]
    for d in range(1, 32):
        total = total + l_recv[d]
    for t in range(4):
        for i in range(4):
            r = 8 * (i % 2) + 2 * t + i // 2
            t_send[t, i : i + 1, :] = total[r : r + 1]
        t_send[t, 4:, :] = total[16:20]
    for t in tp_peers:
        remote(t_send.at[t], t_recv.at[tp], 5, {"tp": t})
    local(t_send.at[tp], t_recv.at[tp], 5)

    finish(sg_recv, recv_sem.at[4])
    finish(t_recv, recv_sem.at[5])
    finish(f_buf.at[:, pl.ds(8, 8 * n_peers), :], send_sem.at[0])
    finish(send.at[pl.ds(0, n_peers)], send_sem.at[1])
    finish(send.at[pl.ds(0, n_peers)], send_sem.at[2])
    finish(l_send.at[pl.ds(0, n_peers)], send_sem.at[3])
    finish(sg_send.at[:, pl.ds(0, n_peers)], send_sem.at[4])
    finish(t_send.at[pl.ds(0, 3)], send_sem.at[5])


def lay_out(sg_in, t_in, sg_out, long_out, short_out):
    swap = swap_matrix(True)
    for g in range(2):
        x = jnp.concatenate(
            [sg_in[32 * g + 16 * h : 32 * g + 16 * (h + 1)].reshape(256, N2) for h in range(2)], axis=1
        )
        y = dot(swap, x).astype(BF16)
        for h in range(2):
            ch = slice(32 * g + 16 * h, 32 * g + 16 * (h + 1))
            for a in range(16):
                sg_out[ch, N2 * a : N2 * (a + 1)] = y[16 * a : 16 * (a + 1), h * N2 : (h + 1) * N2]
    whole = (t_in[0] + t_in[1]) + (t_in[2] + t_in[3])
    long_out[...] = whole[:4]
    short_out[...] = whole[4:5]


def shards(signal, grad_out, long_filter, short_filter, long_skip, short_skip):
    n_ctx, n_tp = lax.axis_size("ctx"), lax.axis_size("tp")
    consts = [jnp.asarray(t) for t in tables()]
    hbm = pl.BlockSpec(memory_space=pltpu.HBM)
    vmem = pl.BlockSpec(memory_space=pltpu.VMEM)
    V, S = pltpu.VMEM, pltpu.SMEM
    spec = V((N1, 2 * N2), F32)
    raw_sg, raw_t = pl.pallas_call(
        lambda *refs: kernel(n_ctx, n_tp, *refs),
        out_shape=(
            jax.ShapeDtypeStruct((64, 16, N2), BF16),
            jax.ShapeDtypeStruct((4, 8, N2), F32),
        ),
        in_specs=[hbm] * 10,
        out_specs=(vmem, vmem),
        scratch_shapes=[
            V((64, 2048), BF16), V((64, 2048), BF16), V((16, N2), F32), V((2, 8, N2), F32),
            V((1, N2), F32), S((64,), F32), S((64,), F32),
            V((2 * N1, N1), BF16), V((N1, 2 * N1), BF16), V((N1, 2 * N2), F32), V((1536, 256), BF16),
            V((64, 2, 16, N2), BF16), V((2, 2, N1, N2), BF16), V((2, HALF + 8, N2), F32),
            spec, spec, spec, spec, spec, spec, V((HALF + 8, N2), F32),
            V((32, 24, N2), F32), V((32, 24, N2), F32), V((4, 8, N2), F32), V((2, 32, 16, N2), BF16),
            pltpu.SemaphoreType.DMA((10,)), pltpu.SemaphoreType.DMA((6,)), pltpu.SemaphoreType.DMA((6,)),
        ],
        compiler_params=pltpu.CompilerParams(
            collective_id=0, has_side_effects=True, vmem_limit_bytes=60 * 1024 * 1024
        ),
        cost_estimate=pl.CostEstimate(flops=6_000_000_000, bytes_accessed=8_000_000, transcendentals=0),
    )(
        signal, grad_out, long_filter.reshape(16, N2), short_filter.reshape(1, N2),
        long_skip, short_skip, *consts,
    )
    sg, long, short = pl.pallas_call(
        lay_out,
        out_shape=(
            jax.ShapeDtypeStruct((64, 2048), BF16),
            jax.ShapeDtypeStruct((4, N2), F32),
            jax.ShapeDtypeStruct((1, N2), F32),
        ),
        in_specs=[vmem, vmem],
        out_specs=(vmem, vmem, vmem),
    )(raw_sg, raw_t)
    return sg, long.reshape(512), short.reshape(N2)


def solution(mesh):
    placed = (P("tp", "ctx"), P("tp", "ctx"), P("ctx"), P(), P("tp"), P("tp"))
    return jax.shard_map(
        shards,
        mesh=mesh,
        in_specs=placed,
        out_specs=(P("tp", "ctx"), P(("ctx", "tp")), P()),
        check_vma=False,
    )
```

```python
import math

import jax
import jax.numpy as jnp
import ml_dtypes
import numpy as np
from jax import lax
from jax.experimental import pallas as pl
from jax.experimental.pallas import tpu as pltpu
from jax.sharding import PartitionSpec as P

MESH = pl.DeviceIdType.MESH
F32, BF16 = jnp.float32, jnp.bfloat16
N1, N2 = 512, 128
LEN = N1 * N2
HALF = N1 // 2


def split_np(x):
    x = x.astype(np.float32)
    hi = x.astype(ml_dtypes.bfloat16)
    lo = (x - hi.astype(np.float32)).astype(ml_dtypes.bfloat16)
    return hi, lo


def tables():
    k = np.arange(N1, dtype=np.float64)[:, None] + 0.25
    kh = k[:HALF]
    fwd, inv = [], []
    for odd in range(2):
        n = 2 * np.arange(HALF, dtype=np.float64)[None, :] + odd
        ang = -2 * np.pi * np.mod(kh * n, N1) / N1
        hi, lo = split_np(np.concatenate([np.cos(ang), np.sin(ang)], axis=0))
        fwd.append(np.concatenate([hi, lo], axis=1))
        inv.append(np.concatenate([hi.T, lo.T], axis=1))
    m = np.arange(N2, dtype=np.float64)
    ang = -2 * np.pi * k * m[None, :] / LEN
    twist = np.concatenate([np.cos(ang), np.sin(ang)], axis=1).astype(np.float32)
    ang = -2 * np.pi * np.mod(m[:, None] * m[None, :], N2) / N2
    br, bi = np.cos(ang), np.sin(ang)
    b_hi, b_lo = split_np(np.block([[br, bi], [-bi, br]]))
    c_hi, c_lo = split_np(np.block([[br, -bi], [bi, br]]) / LEN)
    mix = np.concatenate([b_hi, b_hi, b_lo, c_hi, c_hi, c_lo])
    return np.concatenate(fwd), np.concatenate(inv), twist, mix


def dot(a, b):
    return jnp.dot(a, b, preferred_element_type=F32)


def split(x):
    hi = x.astype(BF16)
    return hi, (x - hi.astype(F32)).astype(BF16)


def split3(x):
    hi, lo = split(x)
    return jnp.concatenate([hi, lo, hi], axis=1)


def twice(x):
    return jnp.concatenate([x, x], axis=0)


def mix_forward(even, odd, twist, mix, z_refs):
    for q, z in enumerate(z_refs):
        s = slice(q * N2, (q + 1) * N2)
        er, ei, dr, di = even[:HALF, s], even[HALF:, s], odd[:HALF, s], odd[HALF:, s]
        for h, (xr, xi) in enumerate([(er + dr, ei + di), (er - dr, ei - di)]):
            r = slice(h * HALF, (h + 1) * HALF)
            tr, ti = twist[r, :N2], twist[r, N2:]
            y = jnp.concatenate([xr * tr - xi * ti, xi * tr + xr * ti], axis=1)
            z[r, :] = dot(split3(y), mix[:768, :])


def forward_exact(xe, xo, fwd, twist, mix, z_refs):
    mix_forward(dot(fwd[:N1, :], twice(xe)), dot(fwd[N1:, :], twice(xo)), twist, mix, z_refs)


def forward_split(xe, xo, fwd, twist, mix, z_refs):
    out = []
    for h, x in enumerate((xe, xo)):
        hi, lo = split(x)
        r = slice(h * N1, (h + 1) * N1)
        out.append(dot(fwd[r, :], twice(hi)) + dot(fwd[r, :HALF], lo))
    mix_forward(out[0], out[1], twist, mix, z_refs)


def inverse_pair(left, right, inv, twist, mix):
    plus, minus = [], []
    for a, b in zip(left, right):
        ys = []
        for h in range(2):
            r = slice(h * HALF, (h + 1) * HALF)
            ar, ai, br, bi = a[r, :N2], a[r, N2:], b[r, :N2], b[r, N2:]
            z = jnp.concatenate([ar * br + ai * bi, ai * br - ar * bi], axis=1)
            y = dot(split3(z), mix[768:, :])
            yr, yi = y[:, :N2], y[:, N2:]
            tr, ti = twist[r, :N2], twist[r, N2:]
            ys.append(jnp.concatenate([yr * tr + yi * ti, yi * tr - yr * ti], axis=0))
        plus.append(ys[0] + ys[1])
        minus.append(ys[0] - ys[1])
    out = []
    for h, y in enumerate((plus, minus)):
        hi, lo = split(jnp.concatenate(y, axis=1))
        r = slice(h * HALF, (h + 1) * HALF)
        out.append(dot(inv[r, :], twice(hi)) + dot(inv[r, :N1], lo))
    return out


def one_hot(cond):
    return jnp.where(cond, 1.0, 0.0).astype(BF16)


def swap_matrix(back):
    i = lax.broadcasted_iota(jnp.int32, (256, 256), 0)
    j = lax.broadcasted_iota(jnp.int32, (256, 256), 1)
    if back:
        i, j = j, i
    p = i % 16
    return one_hot((i // 16 == j % 16) & (2 * (p % 8) + p // 8 == j // 16))


def rolled(w_row, first, rows):
    zero = jnp.zeros((1, N2), F32)
    base = jnp.concatenate([w_row, zero] if first else [zero, w_row], axis=1)
    return pltpu.roll(jnp.broadcast_to(base, (rows, 2 * N2)), 0, 1, stride=1, stride_axis=0)


def stack3(x):
    hi, lo = split(x)
    return jnp.concatenate([hi, hi, lo], axis=0)


def long_rows(re, ro, r_buf, band, alpha):
    se, so = re[0] + re[1], ro[0] + ro[1]
    r_buf[:HALF, :] = se
    pair = jnp.concatenate(
        [jnp.concatenate([se, so], axis=1), jnp.concatenate([so, r_buf[pl.ds(1, HALF), :]], axis=1)], axis=0
    )
    long = dot(split3(pair), band)
    long_e = long[:HALF] + (alpha[0] * re[0] + alpha[1] * re[1])
    long_o = long[HALF:] + (alpha[0] * ro[0] + alpha[1] * ro[1])
    return long_e, long_o, pair


def short_row(pair, f_t, re, lam):
    th, tl = split(f_t)
    ph, plo = split(pair)
    cross = dot(th, ph) + (dot(th, plo) + dot(tl, ph))
    i = lax.broadcasted_iota(jnp.int32, (N2, N2), 0)
    j = lax.broadcasted_iota(jnp.int32, (N2, N2), 1)
    flip = one_hot(i + j == N2 - 1)
    ch, cl = split(cross)
    diag = pltpu.roll(dot(flip, ch) + dot(flip, cl), N2 + 1, 1, stride=1, stride_axis=0)
    short = jnp.sum(diag, axis=0, keepdims=True)[:, :N2]
    return short + (lam[0] * re[0][:1, :] + lam[1] * re[1][:1, :])


def filters(f_buf, w_row, band, alpha, lam):
    fe, fo = f_buf[0, 8:, :], f_buf[1, 8:, :]
    pair = jnp.concatenate(
        [
            jnp.concatenate([f_buf[1, pl.ds(7, HALF), :], fe], axis=1),
            jnp.concatenate([fe, fo], axis=1),
        ],
        axis=0,
    )
    u = dot(split3(pair), band)
    first_row = lax.broadcasted_iota(jnp.int32, (8, N2), 0) == 0
    first = first_row & (lax.broadcasted_iota(jnp.int32, (8, N2), 1) == 0)
    ve, vo = [], []
    for c in range(2):
        v = u[:HALF] + alpha[c] * fe
        extra = jnp.where(first_row, lam[c] * w_row, 0.0) + jnp.where(first, lam[c] * alpha[c], 0.0)
        ve.append(jnp.concatenate([v[:8] + extra, v[8:]], axis=0))
        vo.append(u[HALF:] + alpha[c] * fo)
    return jnp.concatenate(ve, axis=1), jnp.concatenate(vo, axis=1)


def halves(x):
    x = x.astype(F32).reshape(32, 16, N2)
    return x[:, :8].reshape(HALF, N2).astype(BF16), x[:, 8:].reshape(HALF, N2).astype(BF16)


def offsets():
    def far(o):
        return o[0] + min(o[1], 4 - o[1]) + min(o[2], 4 - o[2])

    out = [(y, z, x) for y in range(2) for z in range(4) for x in range(4)][1:]
    return sorted(out, key=lambda o: -far(o))


def kernel(
    n_ctx, n_tp,
    sig, cot, filt, w_in, lam_in, alpha_in, f_tab, i_tab, t_tab, m_tab,
    sg_recv, long_out, short_out,
    sig_v, cot_v, filt_v, filt_s, w_v, lam_s, alpha_s, fwd, inv, twist, mix,
    send, recv, f_buf, zs, zg, zv0, zv1, r_buf, band_a, band_c, f_t,
    l_send, l_recv, s_send, s_recv, sg_send, load_sem, send_sem, recv_sem, ready,
):
    me, tp = lax.axis_index("ctx"), lax.axis_index("tp")
    zv = (zv0, zv1)
    my_y, my_z, my_x = me // 16, (me // 4) % 4, me % 4
    peers = [((my_y + y) % 2) * 16 + ((my_z + z) % 4) * 4 + (my_x + x) % 4 for y, z, x in offsets()]
    tp_peers = [(tp + i) % n_tp for i in (2, 3, 1)]
    n_peers = len(peers)
    n_all = n_ctx * n_tp
    my_id = n_tp * me + tp

    barrier = pltpu.get_barrier_semaphore()
    loads = [
        pltpu.make_async_copy(src, dst, load_sem.at[i])
        for i, (src, dst) in enumerate(
            [(filt, filt_v), (sig, sig_v), (cot, cot_v), (w_in, w_v), (lam_in, lam_s), (alpha_in, alpha_s),
             (f_tab, fwd), (t_tab, twist), (m_tab, mix), (i_tab, inv)]
        )
    ]
    for c in loads:
        c.start()
    for e in peers:
        pl.semaphore_signal(barrier, inc=1, device_id={"ctx": e}, device_id_type=MESH)
    for t in tp_peers:
        pl.semaphore_signal(barrier, inc=1, device_id={"tp": t}, device_id_type=MESH)
    f_buf[:, :8, :] = jnp.zeros((2, 8, N2), F32)
    r_buf[HALF:, :] = jnp.zeros((8, N2), F32)
    swap = swap_matrix(False)
    for c in loads[:6]:
        c.wait()
    for h in range(2):
        for i in range(8):
            filt_s[h, i : i + 1, :] = filt_v[2 * i + h : 2 * i + h + 1, :]
    for g in range(4):
        ch = slice(16 * g, 16 * (g + 1))
        x = jnp.concatenate(
            [
                jnp.concatenate([v[ch, N2 * a : N2 * (a + 1)] for a in range(16)], axis=0)
                for v in (sig_v, cot_v)
            ],
            axis=1,
        )
        y = dot(swap, x).astype(BF16)
        send[ch, 0] = y[:, :N2].reshape(16, 16, N2)
        send[ch, 1] = y[:, N2:].reshape(16, 16, N2)
    w_row = w_v[...]
    band_a[...] = stack3(jnp.transpose(rolled(w_row, True, N2)))
    band_c[...] = stack3(rolled(w_row, False, 2 * N2)[:, :N2])
    alpha = (alpha_s[2 * me], alpha_s[2 * me + 1])
    lam = (lam_s[2 * me], lam_s[2 * me + 1])
    pl.semaphore_wait(barrier, n_peers + len(tp_peers))
    for t in tp_peers:
        pl.semaphore_signal(ready, inc=1, device_id={"tp": t}, device_id_type=MESH)

    rows_me = pl.ds(pl.multiple_of(16 * me, 16), 16)
    f_dst = f_buf.at[:, pl.ds(pl.multiple_of(8 + 8 * me, 8), 8), :]

    def remote(src, dst, k, where):
        pltpu.make_async_remote_copy(
            src_ref=src, dst_ref=dst, send_sem=send_sem.at[k], recv_sem=recv_sem.at[k],
            device_id=where, device_id_type=MESH,
        ).start()

    def local(src, dst, k):
        pltpu.make_async_copy(src, dst, recv_sem.at[k]).start()

    def finish(ref, sem):
        pltpu.make_async_copy(ref, ref, sem).wait()

    for e in peers:
        remote(filt_s, f_dst, 0, {"ctx": e})
    for c in range(2):
        for e in peers:
            remote(send.at[2 * e + c], recv.at[c, :, rows_me, :], 1 + c, {"ctx": e})
    local(filt_s, f_dst, 0)
    for c in range(2):
        local(send.at[2 * me + c], recv.at[c, :, rows_me, :], 1 + c)

    for c in loads[6:]:
        c.wait()
    finish(f_buf.at[:, pl.ds(8, HALF), :], recv_sem.at[0])
    ve, vo = filters(f_buf, w_row, band_c[...], alpha, lam)
    forward_split(ve, vo, fwd, twist, mix, zv)
    f_t[...] = jnp.transpose(jnp.concatenate([f_buf[0, 8:, :], f_buf[1, 8:, :]], axis=0))

    re, ro = [], []
    for c in range(2):
        finish(recv.at[c], recv_sem.at[1 + c])
        se, so = halves(recv[c, 0])
        ge, go = halves(recv[c, 1])
        forward_exact(
            jnp.concatenate([se, ge], axis=1), jnp.concatenate([so, go], axis=1), fwd, twist, mix, (zs, zg)
        )
        even, odd = inverse_pair((zg, zg), (zs, zv[c]), inv, twist, mix)
        re.append(even[:, :N2])
        ro.append(odd[:, :N2])
        rows = [x[:, N2:].reshape(32, 8, N2) for x in (even, odd)]
        sg_send[c] = jnp.concatenate(rows, axis=1).astype(BF16)
        for e in peers:
            remote(sg_send.at[c, e], sg_recv.at[2 * me + c], 3 + c, {"ctx": e})
        local(sg_send.at[c, me], sg_recv.at[2 * me + c], 3 + c)

    long_e, long_o, pair = long_rows(re, ro, r_buf, band_a[...], alpha)
    l_send[pl.ds(0, HALF, 2), :] = long_e
    l_send[pl.ds(1, HALF, 2), :] = long_o
    pl.semaphore_wait(ready, len(tp_peers))
    everyone = [(e, t) for t in tp_peers for e in peers] + [(me, t) for t in tp_peers] + [(e, tp) for e in peers]
    l_dst = l_recv.at[pl.ds(pl.multiple_of(4 * my_id, 4), 4), :]
    for e, t in everyone:
        src = l_send.at[pl.ds(pl.multiple_of(4 * (n_tp * e + t), 4), 4), :]
        remote(src, l_dst, 5, {"ctx": e, "tp": t})
    local(l_send.at[pl.ds(pl.multiple_of(4 * my_id, 4), 4), :], l_dst, 5)

    s_send[...] = short_row(pair, f_t[...], re, lam)
    s_dst = s_recv.at[pl.ds(my_id, 1), :]
    for e, t in everyone:
        remote(s_send, s_dst, 6, {"ctx": e, "tp": t})
    local(s_send, s_dst, 6)

    finish(l_recv, recv_sem.at[5])
    total = jnp.sum(l_recv[...].reshape(64, 8, N2), axis=0)
    long_out[...] = total[:4] + total[4:]
    finish(s_recv, recv_sem.at[6])
    short_out[...] = jnp.sum(s_recv[...], axis=0, keepdims=True)
    for c in range(2):
        finish(sg_send.at[c], recv_sem.at[3 + c])
    finish(f_buf.at[:, pl.ds(8, 8 * n_peers), :], send_sem.at[0])
    finish(send.at[pl.ds(0, n_peers)], send_sem.at[1])
    finish(send.at[pl.ds(0, n_peers)], send_sem.at[2])
    for c in range(2):
        finish(sg_send.at[c, pl.ds(0, n_peers)], send_sem.at[3 + c])
    finish(l_send.at[pl.ds(0, 4 * (n_all - 1)), :], send_sem.at[5])
    finish(s_recv.at[pl.ds(0, n_all - 1), :], send_sem.at[6])


def lay_out(sg_in, long_in, short_in, sg_out, long_out, short_out):
    swap = swap_matrix(True)
    for g in range(2):
        x = jnp.concatenate(
            [sg_in[32 * g + 16 * h : 32 * g + 16 * (h + 1)].reshape(256, N2) for h in range(2)], axis=1
        )
        y = dot(swap, x).astype(BF16)
        for h in range(2):
            ch = slice(32 * g + 16 * h, 32 * g + 16 * (h + 1))
            for a in range(16):
                sg_out[ch, N2 * a : N2 * (a + 1)] = y[16 * a : 16 * (a + 1), h * N2 : (h + 1) * N2]
    long_out[...] = long_in[...]
    short_out[...] = short_in[...]


def shards(signal, grad_out, long_filter, short_filter, long_skip, short_skip):
    n_ctx, n_tp = lax.axis_size("ctx"), lax.axis_size("tp")
    consts = [jnp.asarray(t) for t in tables()]
    hbm = pl.BlockSpec(memory_space=pltpu.HBM)
    vmem = pl.BlockSpec(memory_space=pltpu.VMEM)
    V, S = pltpu.VMEM, pltpu.SMEM
    spec = V((N1, 2 * N2), F32)
    raw = pl.pallas_call(
        lambda *refs: kernel(n_ctx, n_tp, *refs),
        out_shape=(
            jax.ShapeDtypeStruct((64, 16, N2), BF16),
            jax.ShapeDtypeStruct((4, N2), F32),
            jax.ShapeDtypeStruct((1, N2), F32),
        ),
        in_specs=[hbm] * 10,
        out_specs=(vmem, vmem, vmem),
        scratch_shapes=[
            V((64, 2048), BF16), V((64, 2048), BF16), V((16, N2), F32), V((2, 8, N2), F32),
            V((1, N2), F32), S((64,), F32), S((64,), F32),
            V((2 * N1, N1), BF16), V((N1, 2 * N1), BF16), V((N1, 2 * N2), F32), V((1536, 256), BF16),
            V((64, 2, 16, N2), BF16), V((2, 2, N1, N2), BF16), V((2, HALF + 8, N2), F32),
            spec, spec, spec, spec, V((HALF + 8, N2), F32),
            V((768, N2), BF16), V((768, N2), BF16), V((N2, N1), F32),
            V((N1, N2), F32), V((N1, N2), F32), V((1, N2), F32), V((128, N2), F32), V((2, 32, 16, N2), BF16),
            pltpu.SemaphoreType.DMA((10,)), pltpu.SemaphoreType.DMA((7,)), pltpu.SemaphoreType.DMA((7,)),
            pltpu.SemaphoreType.REGULAR,
        ],
        compiler_params=pltpu.CompilerParams(
            collective_id=0, has_side_effects=True, vmem_limit_bytes=60 * 1024 * 1024
        ),
        cost_estimate=pl.CostEstimate(flops=6_000_000_000, bytes_accessed=8_000_000, transcendentals=0),
    )(
        signal, grad_out, long_filter.reshape(16, N2), short_filter.reshape(1, N2),
        long_skip, short_skip, *consts,
    )
    sg, long, short = pl.pallas_call(
        lay_out,
        out_shape=(
            jax.ShapeDtypeStruct((64, 2048), BF16),
            jax.ShapeDtypeStruct((4, N2), F32),
            jax.ShapeDtypeStruct((1, N2), F32),
        ),
        in_specs=[vmem, vmem, vmem],
        out_specs=(vmem, vmem, vmem),
    )(*raw)
    return sg, long.reshape(512), short.reshape(N2)


def solution(mesh):
    placed = (P("tp", "ctx"), P("tp", "ctx"), P("ctx"), P(), P("tp"), P("tp"))
    return jax.shard_map(
        shards,
        mesh=mesh,
        in_specs=placed,
        out_specs=(P("tp", "ctx"), P(("ctx", "tp")), P()),
        check_vma=False,
    )
```

```python
import math

import jax
import jax.numpy as jnp
import ml_dtypes
import numpy as np
from jax import lax
from jax.experimental import pallas as pl
from jax.experimental.pallas import tpu as pltpu
from jax.sharding import PartitionSpec as P

MESH = pl.DeviceIdType.MESH
F32, BF16 = jnp.float32, jnp.bfloat16
N1, N2 = 512, 128
LEN = N1 * N2
HALF = N1 // 2


def split_np(x):
    x = x.astype(np.float32)
    hi = x.astype(ml_dtypes.bfloat16)
    lo = (x - hi.astype(np.float32)).astype(ml_dtypes.bfloat16)
    return hi, lo


def tables():
    k = np.arange(N1, dtype=np.float64)[:, None] + 0.25
    kh = k[:HALF]
    fwd, inv = [], []
    for odd in range(2):
        n = 2 * np.arange(HALF, dtype=np.float64)[None, :] + odd
        ang = -2 * np.pi * np.mod(kh * n, N1) / N1
        hi, lo = split_np(np.concatenate([np.cos(ang), np.sin(ang)], axis=0))
        fwd.append(np.concatenate([hi, lo], axis=1))
        inv.append(np.concatenate([hi.T, lo.T], axis=1))
    m = np.arange(N2, dtype=np.float64)
    ang = -2 * np.pi * k * m[None, :] / LEN
    twist = np.concatenate([np.cos(ang), np.sin(ang)], axis=1)
    ang = np.broadcast_to(-2 * np.pi * kh / N1, (HALF, N2))
    twist = np.concatenate([twist, np.concatenate([np.cos(ang), np.sin(ang)], axis=1)]).astype(np.float32)
    ang = -2 * np.pi * np.mod(m[:, None] * m[None, :], N2) / N2
    br, bi = np.cos(ang), np.sin(ang)
    b_hi, b_lo = split_np(np.block([[br, bi], [-bi, br]]))
    c_hi, c_lo = split_np(np.block([[br, -bi], [bi, br]]) / LEN)
    mix = np.concatenate([b_hi, b_hi, b_lo, c_hi, c_hi, c_lo])
    return np.concatenate(fwd), np.concatenate(inv), twist, mix


def dot(a, b):
    return jnp.dot(a, b, preferred_element_type=F32)


def split(x):
    hi = x.astype(BF16)
    return hi, (x - hi.astype(F32)).astype(BF16)


def split3(x):
    hi, lo = split(x)
    return jnp.concatenate([hi, lo, hi], axis=1)


def twice(x):
    return jnp.concatenate([x, x], axis=0)


def mix_forward(even, odd, twist, mix, z_refs):
    for q, z in enumerate(z_refs):
        s = slice(q * N2, (q + 1) * N2)
        er, ei, dr, di = even[:HALF, s], even[HALF:, s], odd[:HALF, s], odd[HALF:, s]
        for h, (xr, xi) in enumerate([(er + dr, ei + di), (er - dr, ei - di)]):
            r = slice(h * HALF, (h + 1) * HALF)
            tr, ti = twist[r, :N2], twist[r, N2:]
            y = jnp.concatenate([xr * tr - xi * ti, xi * tr + xr * ti], axis=1)
            z[r, :] = dot(split3(y), mix[:768, :])


def forward_exact(xe, xo, fwd, twist, mix, z_refs):
    mix_forward(dot(fwd[:N1, :], twice(xe)), dot(fwd[N1:, :], twice(xo)), twist, mix, z_refs)


def forward_filter(fe, fo, fwd, twist, mix, z):
    hi, lo = split(jnp.concatenate([fe, fo], axis=1))
    y = dot(fwd[:N1, :], twice(hi)) + dot(fwd[:N1, :HALF], lo)
    tr, ti = twist[N1:, :N2], twist[N1:, N2:]
    dr, di = y[:HALF, N2:], y[HALF:, N2:]
    odd = jnp.concatenate([dr * tr - di * ti, di * tr + dr * ti], axis=0)
    mix_forward(y[:, :N2], odd, twist, mix, (z,))


def inverse_pair(left, right, inv, twist, mix):
    plus, minus = [], []
    for a, b in zip(left, right):
        ys = []
        for h in range(2):
            r = slice(h * HALF, (h + 1) * HALF)
            ar, ai = a[r, :N2], a[r, N2:]
            br, bi = b(r)
            z = jnp.concatenate([ar * br + ai * bi, ai * br - ar * bi], axis=1)
            y = dot(split3(z), mix[768:, :])
            yr, yi = y[:, :N2], y[:, N2:]
            tr, ti = twist[r, :N2], twist[r, N2:]
            ys.append(jnp.concatenate([yr * tr + yi * ti, yi * tr - yr * ti], axis=0))
        plus.append(ys[0] + ys[1])
        minus.append(ys[0] - ys[1])
    out = []
    for h, y in enumerate((plus, minus)):
        hi, lo = split(jnp.concatenate(y, axis=1))
        r = slice(h * HALF, (h + 1) * HALF)
        out.append(dot(inv[r, :], twice(hi)) + dot(inv[r, :N1], lo))
    return out


def one_hot(cond):
    return jnp.where(cond, 1.0, 0.0).astype(BF16)


def swap_matrix(back):
    i = lax.broadcasted_iota(jnp.int32, (256, 256), 0)
    j = lax.broadcasted_iota(jnp.int32, (256, 256), 1)
    if back:
        i, j = j, i
    p = i % 16
    return one_hot((i // 16 == j % 16) & (2 * (p % 8) + p // 8 == j // 16))


def rolled(w_row, first, rows):
    zero = jnp.zeros((1, N2), F32)
    base = jnp.concatenate([w_row, zero] if first else [zero, w_row], axis=1)
    return pltpu.roll(jnp.broadcast_to(base, (rows, 2 * N2)), 0, 1, stride=1, stride_axis=0)


def stack3(x):
    hi, lo = split(x)
    return jnp.concatenate([hi, hi, lo], axis=0)


def long_rows(re, ro, r_buf, band, alpha):
    se, so = re[0] + re[1], ro[0] + ro[1]
    r_buf[:HALF, :] = se
    pair = jnp.concatenate(
        [jnp.concatenate([se, so], axis=1), jnp.concatenate([so, r_buf[pl.ds(1, HALF), :]], axis=1)], axis=0
    )
    long = dot(split3(pair), band)
    long_e = long[:HALF] + (alpha[0] * re[0] + alpha[1] * re[1])
    long_o = long[HALF:] + (alpha[0] * ro[0] + alpha[1] * ro[1])
    return long_e, long_o, pair


def turned_filter(fe, fo):
    i = lax.broadcasted_iota(jnp.int32, (N2, N2), 0)
    j = lax.broadcasted_iota(jnp.int32, (N2, N2), 1)
    flip = one_hot(i + j == N2 - 1)
    hi, lo = split(jnp.transpose(jnp.concatenate([fe, fo], axis=0)))
    return dot(flip, hi).astype(BF16), dot(flip, lo).astype(BF16)


def short_row(pair, f_hi, f_lo, re, lam):
    hi, lo = split(pair)
    cross = dot(f_hi, hi) + (dot(f_hi, lo) + dot(f_lo, hi))
    diag = pltpu.roll(cross, N2 + 1, 1, stride=1, stride_axis=0)
    short = jnp.sum(diag, axis=0, keepdims=True)[:, :N2]
    return short + (lam[0] * re[0][:1, :] + lam[1] * re[1][:1, :])


def whole(z):
    return lambda r: (z[r, :N2], z[r, N2:])


def filter_product(zf, zw, lam, alpha):
    def rows(r):
        fr, fi = zf[r, :N2] + lam, zf[r, N2:]
        wr, wi = zw[r, :N2] + alpha, zw[r, N2:]
        return fr * wr - fi * wi, fr * wi + fi * wr

    return rows


def tail_matrix(f_last, band):
    tail = dot(split3(f_last), band)
    i = lax.broadcasted_iota(jnp.int32, (N2, N2), 0)
    j = lax.broadcasted_iota(jnp.int32, (N2, N2), 1)
    flip = one_hot(i + j == N2)
    hi, lo = split(tail)
    turned = (dot(hi, flip) + dot(lo, flip))[7:, :]
    return rolled(turned, True, N2)[:, :N2]


def halves(x):
    x = x.astype(F32).reshape(32, 16, N2)
    return x[:, :8].reshape(HALF, N2).astype(BF16), x[:, 8:].reshape(HALF, N2).astype(BF16)


def offsets():
    def far(o):
        return o[0] + min(o[1], 4 - o[1]) + min(o[2], 4 - o[2])

    out = [(y, z, x) for y in range(2) for z in range(4) for x in range(4)][1:]
    return sorted(out, key=lambda o: -far(o))


def all_offsets():
    def far(o):
        y = (1 if o[1] else 2) if o[0] & 2 else o[1]
        return y + min(o[2], 4 - o[2]) + min(o[3], 4 - o[3])

    out = [(t, y, z, x) for y in range(2) for z in range(4) for x in range(4) for t in range(4)][1:]
    return sorted(out, key=lambda o: -far(o))


def kernel(
    n_ctx, n_tp,
    sig, cot, filt, w_in, lam_in, alpha_in, f_tab, i_tab, t_tab, m_tab,
    sg_recv, long_out, short_out,
    sig_v, cot_v, filt_v, filt_s, w_v, lam_s, alpha_s, fwd, inv, twist, mix,
    send, recv, f_buf, zs0, zg0, zs1, zg1, zf, r_buf, band_a, band_c, zw,
    l_rows, l_send, l_recv, s_send, s_recv, sg_send, load_sem, send_sem, recv_sem, ready,
):
    me, tp = lax.axis_index("ctx"), lax.axis_index("tp")
    zs, zg = (zs0, zs1), (zg0, zg1)
    my_y, my_z, my_x = me // 16, (me // 4) % 4, me % 4
    at = {(y, z, x): (my_y ^ y) * 16 + ((my_z + z) & 3) * 4 + ((my_x + x) & 3) for y, z, x in [(0, 0, 0)] + offsets()}
    peers = [at[o] for o in offsets()]
    tp_peers = [tp ^ i for i in (3, 2, 1)]
    n_peers = len(peers)
    n_all = n_ctx * n_tp
    my_id = n_tp * me + tp

    barrier = pltpu.get_barrier_semaphore()
    for e in peers:
        pl.semaphore_signal(barrier, inc=1, device_id={"ctx": e}, device_id_type=MESH)
    for t in tp_peers:
        pl.semaphore_signal(barrier, inc=1, device_id={"tp": t}, device_id_type=MESH)
    loads = [
        pltpu.make_async_copy(src, dst, load_sem.at[i])
        for i, (src, dst) in enumerate(
            [(filt, filt_v), (sig, sig_v), (cot, cot_v), (w_in, w_v), (lam_in, lam_s), (alpha_in, alpha_s),
             (f_tab, fwd), (t_tab, twist), (m_tab, mix), (i_tab, inv)]
        )
    ]
    for c in loads:
        c.start()
    r_buf[HALF:, :] = jnp.zeros((8, N2), F32)
    swap = swap_matrix(False)
    for c in loads[:6]:
        c.wait()
    for h in range(2):
        for i in range(8):
            filt_s[h, i : i + 1, :] = filt_v[2 * i + h : 2 * i + h + 1, :]
    for g in range(4):
        ch = slice(16 * g, 16 * (g + 1))
        x = jnp.concatenate(
            [
                jnp.concatenate([v[ch, N2 * a : N2 * (a + 1)] for a in range(16)], axis=0)
                for v in (sig_v, cot_v)
            ],
            axis=1,
        )
        y = dot(swap, x).astype(BF16)
        send[ch, 0] = y[:, :N2].reshape(16, 16, N2)
        send[ch, 1] = y[:, N2:].reshape(16, 16, N2)
    pl.semaphore_wait(barrier, n_peers + len(tp_peers))
    for t in tp_peers:
        pl.semaphore_signal(ready, inc=1, device_id={"tp": t}, device_id_type=MESH)

    rows_me = pl.ds(pl.multiple_of(16 * me, 16), 16)
    f_dst = f_buf.at[:, pl.ds(pl.multiple_of(8 * me, 8), 8), :]

    def remote(src, dst, k, where):
        pltpu.make_async_remote_copy(
            src_ref=src, dst_ref=dst, send_sem=send_sem.at[k], recv_sem=recv_sem.at[k],
            device_id=where, device_id_type=MESH,
        ).start()

    def local(src, dst, k):
        pltpu.make_async_copy(src, dst, recv_sem.at[k]).start()

    def finish(ref, sem):
        pltpu.make_async_copy(ref, ref, sem).wait()

    for c in range(2):
        for e in peers:
            remote(send.at[2 * e + c], recv.at[c, :, rows_me, :], 1 + c, {"ctx": e})
    for e in peers:
        remote(filt_s, f_dst, 0, {"ctx": e})
    for c in range(2):
        local(send.at[2 * me + c], recv.at[c, :, rows_me, :], 1 + c)
    local(filt_s, f_dst, 0)

    w_row = w_v[...]
    band_a[...] = stack3(jnp.transpose(rolled(w_row, True, N2)))
    band_c[...] = stack3(rolled(w_row, False, N2)[:, :N2])
    alpha = (alpha_s[2 * me], alpha_s[2 * me + 1])
    lam = (lam_s[2 * me], lam_s[2 * me + 1])
    for c in loads[6:]:
        c.wait()
    zw[...] = dot(split3(twist[:N1, :] * jnp.concatenate([w_row, w_row], axis=1)), mix[:768, :])

    for c in range(2):
        finish(recv.at[c], recv_sem.at[1 + c])
        se, so = halves(recv[c, 0])
        ge, go = halves(recv[c, 1])
        forward_exact(
            jnp.concatenate([se, ge], axis=1), jnp.concatenate([so, go], axis=1), fwd, twist, mix, (zs[c], zg[c])
        )
    even, odd = inverse_pair(zg, [whole(z) for z in zs], inv, twist, mix)
    re, ro = (even[:, :N2], even[:, N2:]), (odd[:, :N2], odd[:, N2:])
    long_e, long_o, pair = long_rows(re, ro, r_buf, band_a[...], alpha)
    l_rows[pl.ds(0, HALF, 2), :] = long_e
    l_rows[pl.ds(1, HALF, 2), :] = long_o
    l_send[...] = l_rows[...].reshape(128, 4, N2)
    pl.semaphore_wait(ready, len(tp_peers))
    everyone = [(at[o[1:]], tp ^ o[0]) for o in all_offsets()]
    for e, t in everyone:
        remote(l_send.at[n_tp * e + t], l_recv.at[my_id], 5, {"ctx": e, "tp": t})
    local(l_send.at[my_id], l_recv.at[my_id], 5)

    finish(f_buf, recv_sem.at[0])
    fe, fo = f_buf[0], f_buf[1]
    ft_hi, ft_lo = turned_filter(fe, fo)
    s_send[...] = short_row(pair, ft_hi, ft_lo, re, lam)
    for e, t in everyone:
        remote(s_send, s_recv.at[my_id], 6, {"ctx": e, "tp": t})
    local(s_send, s_recv.at[my_id], 6)
    forward_filter(fe, fo, fwd, twist, mix, zf)
    t_hi, t_lo = split(tail_matrix(fo[HALF - 8 :, :], band_c[...]))
    even, odd = inverse_pair(
        zg, [filter_product(zf, zw, lam[c], alpha[c]) for c in range(2)], inv, twist, mix
    )
    for c in range(2):
        s = slice(c * N2, (c + 1) * N2)
        first = recv[c, 1, :16, :]
        fold = (dot(first, t_hi) + dot(first, t_lo))[:1, :]
        last = jnp.concatenate([odd[: HALF - 1, s], odd[HALF - 1 :, s] + fold], axis=0)
        rows = [x.reshape(32, 8, N2) for x in (even[:, s], last)]
        sg_send[c] = jnp.concatenate(rows, axis=1).astype(BF16)
    sg_dst = sg_recv.at[pl.ds(2 * me, 2)]
    for e in peers:
        remote(sg_send.at[:, e], sg_dst, 3, {"ctx": e})
    local(sg_send.at[:, me], sg_dst, 3)

    finish(l_recv, recv_sem.at[5])
    long_out[...] = jnp.sum(l_recv[...], axis=0)
    finish(s_recv, recv_sem.at[6])
    short_out[...] = jnp.sum(s_recv[...], axis=0)
    finish(sg_recv, recv_sem.at[3])
    finish(f_buf.at[:, pl.ds(0, 8 * n_peers), :], send_sem.at[0])
    for c in range(2):
        finish(send.at[pl.ds(0, n_peers)], send_sem.at[1 + c])
    finish(sg_send.at[:, pl.ds(0, n_peers)], send_sem.at[3])
    finish(l_send.at[pl.ds(0, n_all - 1)], send_sem.at[5])
    finish(s_recv.at[pl.ds(0, n_all - 1)], send_sem.at[6])


def lay_out(sg_in, long_in, short_in, sg_out, long_out, short_out, rows, sem):
    swap = swap_matrix(True)
    copies = [
        pltpu.make_async_copy(long_in, long_out, sem.at[2]),
        pltpu.make_async_copy(short_in, short_out, sem.at[3]),
    ]
    for c in copies:
        c.start()
    for g in range(2):
        x = jnp.concatenate(
            [sg_in[32 * g + 16 * h : 32 * g + 16 * (h + 1)].reshape(256, N2) for h in range(2)], axis=1
        )
        y = dot(swap, x).astype(BF16)
        for h in range(2):
            ch = slice(32 * g + 16 * h, 32 * g + 16 * (h + 1))
            for a in range(16):
                rows[ch, N2 * a : N2 * (a + 1)] = y[16 * a : 16 * (a + 1), h * N2 : (h + 1) * N2]
        part = pl.ds(32 * g, 32)
        copies.append(pltpu.make_async_copy(rows.at[part, :], sg_out.at[part, :], sem.at[g]))
        copies[-1].start()
    for c in copies:
        c.wait()


def shards(signal, grad_out, long_filter, short_filter, long_skip, short_skip):
    n_ctx, n_tp = lax.axis_size("ctx"), lax.axis_size("tp")
    consts = [jnp.asarray(t) for t in tables()]
    hbm = pl.BlockSpec(memory_space=pltpu.HBM)
    vmem = pl.BlockSpec(memory_space=pltpu.VMEM)
    V, S = pltpu.VMEM, pltpu.SMEM
    spec = V((N1, 2 * N2), F32)
    raw = pl.pallas_call(
        lambda *refs: kernel(n_ctx, n_tp, *refs),
        out_shape=(
            pltpu.VMEM((64, 16, N2), BF16),
            pltpu.VMEM((4, N2), F32),
            pltpu.VMEM((1, N2), F32),
        ),
        in_specs=[hbm] * 10,
        out_specs=(vmem, vmem, vmem),
        scratch_shapes=[
            V((64, 2048), BF16), V((64, 2048), BF16), V((16, N2), F32), V((2, 8, N2), F32),
            V((1, N2), F32), S((64,), F32), S((64,), F32),
            V((2 * N1, N1), BF16), V((N1, 2 * N1), BF16), V((768, 2 * N2), F32), V((1536, 256), BF16),
            V((64, 2, 16, N2), BF16), V((2, 2, N1, N2), BF16), V((2, HALF, N2), F32),
            spec, spec, spec, spec, spec, V((HALF + 8, N2), F32),
            V((768, N2), BF16), V((384, N2), BF16), spec,
            V((N1, N2), F32), V((128, 4, N2), F32), V((128, 4, N2), F32), V((1, N2), F32), V((128, 1, N2), F32), V((2, 32, 16, N2), BF16),
            pltpu.SemaphoreType.DMA((10,)), pltpu.SemaphoreType.DMA((7,)), pltpu.SemaphoreType.DMA((7,)),
            pltpu.SemaphoreType.REGULAR,
        ],
        compiler_params=pltpu.CompilerParams(
            collective_id=0, has_side_effects=True, vmem_limit_bytes=60 * 1024 * 1024
        ),
        cost_estimate=pl.CostEstimate(flops=6_000_000_000, bytes_accessed=8_000_000, transcendentals=0),
    )(
        signal, grad_out, long_filter.reshape(16, N2), short_filter.reshape(1, N2),
        long_skip, short_skip, *consts,
    )
    sg, long, short = pl.pallas_call(
        lay_out,
        out_shape=(
            jax.ShapeDtypeStruct((64, 2048), BF16),
            jax.ShapeDtypeStruct((4, N2), F32),
            jax.ShapeDtypeStruct((1, N2), F32),
        ),
        in_specs=[vmem, vmem, vmem],
        out_specs=(hbm, hbm, hbm),
        scratch_shapes=[V((64, 2048), BF16), pltpu.SemaphoreType.DMA((4,))],
    )(*[pltpu.with_memory_space_constraint(r, pltpu.VMEM) for r in raw])
    return sg, long.reshape(512), short.reshape(N2)


def solution(mesh):
    placed = (P("tp", "ctx"), P("tp", "ctx"), P("ctx"), P(), P("tp"), P("tp"))
    return jax.shard_map(
        shards,
        mesh=mesh,
        in_specs=placed,
        out_specs=(P("tp", "ctx"), P(("ctx", "tp")), P()),
        check_vma=False,
    )
```

```python
import math

import jax
import jax.numpy as jnp
import ml_dtypes
import numpy as np
from jax import lax
from jax.experimental import pallas as pl
from jax.experimental.pallas import tpu as pltpu
from jax.sharding import PartitionSpec as P

MESH = pl.DeviceIdType.MESH
F32, BF16 = jnp.float32, jnp.bfloat16
N1, N2 = 512, 128
LEN = N1 * N2
HALF = N1 // 2


def split_np(x):
    x = x.astype(np.float32)
    hi = x.astype(ml_dtypes.bfloat16)
    lo = (x - hi.astype(np.float32)).astype(ml_dtypes.bfloat16)
    return hi, lo


def tables():
    k = np.arange(N1, dtype=np.float64)[:, None] + 0.25
    kh = k[:HALF]
    fwd, inv = [], []
    for odd in range(2):
        n = 2 * np.arange(HALF, dtype=np.float64)[None, :] + odd
        ang = -2 * np.pi * np.mod(kh * n, N1) / N1
        hi, lo = split_np(np.concatenate([np.cos(ang), np.sin(ang)], axis=0))
        fwd.append(np.concatenate([hi, lo], axis=1))
        inv.append(np.concatenate([hi.T, lo.T], axis=1))
    m = np.arange(N2, dtype=np.float64)
    ang = -2 * np.pi * k * m[None, :] / LEN
    twist = np.concatenate([np.cos(ang), np.sin(ang)], axis=1)
    ang = np.broadcast_to(-2 * np.pi * kh / N1, (HALF, N2))
    twist = np.concatenate([twist, np.concatenate([np.cos(ang), np.sin(ang)], axis=1)]).astype(np.float32)
    ang = -2 * np.pi * np.mod(m[:, None] * m[None, :], N2) / N2
    br, bi = np.cos(ang), np.sin(ang)
    b_hi, b_lo = split_np(np.block([[br, bi], [-bi, br]]))
    c_hi, c_lo = split_np(np.block([[br, -bi], [bi, br]]) / LEN)
    mix = np.concatenate([b_hi, b_hi, b_lo, c_hi, c_hi, c_lo])
    return np.concatenate(fwd), np.concatenate(inv), twist, mix


def dot(a, b):
    return jnp.dot(a, b, preferred_element_type=F32)


def split(x):
    hi = x.astype(BF16)
    return hi, (x - hi.astype(F32)).astype(BF16)


def split3(x):
    hi, lo = split(x)
    return jnp.concatenate([hi, lo, hi], axis=1)


def twice(x):
    return jnp.concatenate([x, x], axis=0)


def mix_forward(even, odd, twist, mix, z_refs):
    for q, z in enumerate(z_refs):
        s = slice(q * N2, (q + 1) * N2)
        er, ei, dr, di = even[:HALF, s], even[HALF:, s], odd[:HALF, s], odd[HALF:, s]
        for h, (xr, xi) in enumerate([(er + dr, ei + di), (er - dr, ei - di)]):
            r = slice(h * HALF, (h + 1) * HALF)
            tr, ti = twist[r, :N2], twist[r, N2:]
            y = jnp.concatenate([xr * tr - xi * ti, xi * tr + xr * ti], axis=1)
            z[r, :] = dot(split3(y), mix[:768, :])


def forward_exact(xe, xo, fwd, twist, mix, z_refs):
    mix_forward(dot(fwd[:N1, :], twice(xe)), dot(fwd[N1:, :], twice(xo)), twist, mix, z_refs)


def forward_filter(fe, fo, fwd, twist, mix, z):
    hi, lo = split(jnp.concatenate([fe, fo], axis=1))
    yr, yi = (dot(fwd[r, :], twice(hi)) + dot(fwd[r, :HALF], lo) for r in (slice(0, HALF), slice(HALF, N1)))
    tr, ti = twist[N1:, :N2], twist[N1:, N2:]
    dr, di = yr[:, N2:], yi[:, N2:]
    even = jnp.concatenate([yr[:, :N2], yi[:, :N2]], axis=0)
    odd = jnp.concatenate([dr * tr - di * ti, di * tr + dr * ti], axis=0)
    mix_forward(even, odd, twist, mix, (z,))


def inverse_mix(a, b, twist, mix):
    ys = []
    for h in range(2):
        r = slice(h * HALF, (h + 1) * HALF)
        ar, ai, br, bi = a[r, :N2], a[r, N2:], b[r, :N2], b[r, N2:]
        z = jnp.concatenate([ar * br + ai * bi, ai * br - ar * bi], axis=1)
        y = dot(split3(z), mix[768:, :])
        yr, yi = y[:, :N2], y[:, N2:]
        tr, ti = twist[r, :N2], twist[r, N2:]
        ys.append(jnp.concatenate([yr * tr + yi * ti, yi * tr - yr * ti], axis=0))
    return ys[0] + ys[1], ys[0] - ys[1]


def inverse_rows(halves, inv):
    out = []
    for h in range(2):
        hi, lo = split(jnp.concatenate([x[h] for x in halves], axis=1))
        r = slice(h * HALF, (h + 1) * HALF)
        out.append(dot(inv[r, :], twice(hi)) + dot(inv[r, :N1], lo))
    return out


def one_hot(cond):
    return jnp.where(cond, 1.0, 0.0).astype(BF16)


def swap_matrix(back):
    i = lax.broadcasted_iota(jnp.int32, (256, 256), 0)
    j = lax.broadcasted_iota(jnp.int32, (256, 256), 1)
    if back:
        i, j = j, i
    p = i % 16
    return one_hot((i // 16 == j % 16) & (2 * (p % 8) + p // 8 == j // 16))


def rolled(w_row, first, rows):
    zero = jnp.zeros((1, N2), F32)
    base = jnp.concatenate([w_row, zero] if first else [zero, w_row], axis=1)
    return pltpu.roll(jnp.broadcast_to(base, (rows, 2 * N2)), 0, 1, stride=1, stride_axis=0)


def stack3(x):
    hi, lo = split(x)
    return jnp.concatenate([hi, hi, lo], axis=0)


def long_rows(re, ro, r_buf, band, alpha):
    se, so = re[0] + re[1], ro[0] + ro[1]
    r_buf[:HALF, :] = se
    pair = jnp.concatenate(
        [jnp.concatenate([se, so], axis=1), jnp.concatenate([so, r_buf[pl.ds(1, HALF), :]], axis=1)], axis=0
    )
    long = dot(split3(pair), band)
    long_e = long[:HALF] + (alpha[0] * re[0] + alpha[1] * re[1])
    long_o = long[HALF:] + (alpha[0] * ro[0] + alpha[1] * ro[1])
    return long_e, long_o, pair


def turned_filter(fe, fo):
    i = lax.broadcasted_iota(jnp.int32, (N2, N2), 0)
    j = lax.broadcasted_iota(jnp.int32, (N2, N2), 1)
    flip = one_hot(i + j == N2 - 1)
    hi, lo = split(jnp.transpose(jnp.concatenate([fe, fo], axis=0)))
    return dot(flip, hi).astype(BF16), dot(flip, lo).astype(BF16)


def short_row(pair, f_hi, f_lo, re, lam):
    hi, lo = split(pair)
    cross = dot(f_hi, hi) + (dot(f_hi, lo) + dot(f_lo, hi))
    diag = pltpu.roll(cross, N2 + 1, 1, stride=1, stride_axis=0)
    short = jnp.sum(diag, axis=0, keepdims=True)[:, :N2]
    return short + (lam[0] * re[0][:1, :] + lam[1] * re[1][:1, :])


def filter_product(zf, zw, lam, alpha, zv):
    fr, fi = zf[:, :N2] + lam, zf[:, N2:]
    wr, wi = zw[:, :N2] + alpha, zw[:, N2:]
    zv[:, :N2] = fr * wr - fi * wi
    zv[:, N2:] = fr * wi + fi * wr


def tail_matrix(f_last, band):
    tail = dot(split3(f_last), band)
    i = lax.broadcasted_iota(jnp.int32, (N2, N2), 0)
    j = lax.broadcasted_iota(jnp.int32, (N2, N2), 1)
    flip = one_hot(i + j == N2)
    hi, lo = split(tail)
    turned = (dot(hi, flip) + dot(lo, flip))[7:, :]
    return rolled(turned, True, N2)[:, :N2]


def halves(x):
    x = x.astype(F32).reshape(32, 16, N2)
    return x[:, :8].reshape(HALF, N2).astype(BF16), x[:, 8:].reshape(HALF, N2).astype(BF16)


def offsets():
    def far(o):
        return o[0] + min(o[1], 4 - o[1]) + min(o[2], 4 - o[2])

    out = [(y, z, x) for y in range(2) for z in range(4) for x in range(4)][1:]
    return sorted(out, key=lambda o: -far(o))


def all_offsets():
    def far(o):
        y = (1 if o[1] else 2) if o[0] & 2 else o[1]
        return y + min(o[2], 4 - o[2]) + min(o[3], 4 - o[3])

    out = [(t, y, z, x) for y in range(2) for z in range(4) for x in range(4) for t in range(4)][1:]
    return sorted(out, key=lambda o: -far(o))


def kernel(
    n_ctx, n_tp,
    sig, cot, filt, w_in, lam_in, alpha_in, f_tab, i_tab, t_tab, m_tab,
    sg_recv, long_out, short_out,
    sig_v, cot_v, filt_v, filt_s, w_v, lam_s, alpha_s, fwd, inv, twist, mix,
    send, recv, f_buf, zs0, zg0, zs1, zg1, zf, zv0, zv1, half, r_buf, band_a, band_c, zw,
    l_rows, l_send, l_recv, s_send, s_recv, sg_send, load_sem, send_sem, recv_sem, ready,
):
    me, tp = lax.axis_index("ctx"), lax.axis_index("tp")
    zs, zg, zv = (zs0, zs1), (zg0, zg1), (zv0, zv1)
    my_y, my_z, my_x = me // 16, (me // 4) % 4, me % 4
    at = {(y, z, x): (my_y ^ y) * 16 + ((my_z + z) & 3) * 4 + ((my_x + x) & 3) for y, z, x in [(0, 0, 0)] + offsets()}
    peers = [at[o] for o in offsets()]
    tp_peers = [tp ^ i for i in (3, 2, 1)]
    n_peers = len(peers)
    n_all = n_ctx * n_tp
    my_id = n_tp * me + tp

    barrier = pltpu.get_barrier_semaphore()
    for e in peers:
        pl.semaphore_signal(barrier, inc=1, device_id={"ctx": e}, device_id_type=MESH)
    for t in tp_peers:
        pl.semaphore_signal(barrier, inc=1, device_id={"tp": t}, device_id_type=MESH)
    loads = [
        pltpu.make_async_copy(src, dst, load_sem.at[i])
        for i, (src, dst) in enumerate(
            [(filt, filt_v), (sig, sig_v), (cot, cot_v), (w_in, w_v), (lam_in, lam_s), (alpha_in, alpha_s),
             (f_tab, fwd), (t_tab, twist), (m_tab, mix), (i_tab, inv)]
        )
    ]
    for c in loads:
        c.start()
    r_buf[HALF:, :] = jnp.zeros((8, N2), F32)
    swap = swap_matrix(False)
    for c in loads[:6]:
        c.wait()
    for h in range(2):
        for i in range(8):
            filt_s[h, i : i + 1, :] = filt_v[2 * i + h : 2 * i + h + 1, :]
    for g in range(4):
        ch = slice(16 * g, 16 * (g + 1))
        x = jnp.concatenate(
            [
                jnp.concatenate([v[ch, N2 * a : N2 * (a + 1)] for a in range(16)], axis=0)
                for v in (sig_v, cot_v)
            ],
            axis=1,
        )
        y = dot(swap, x).astype(BF16)
        send[ch, 0] = y[:, :N2].reshape(16, 16, N2)
        send[ch, 1] = y[:, N2:].reshape(16, 16, N2)
    pl.semaphore_wait(barrier, n_peers + len(tp_peers))
    for t in tp_peers:
        pl.semaphore_signal(ready, inc=1, device_id={"tp": t}, device_id_type=MESH)

    rows_me = pl.ds(pl.multiple_of(16 * me, 16), 16)
    f_dst = f_buf.at[:, pl.ds(pl.multiple_of(8 * me, 8), 8), :]

    def remote(src, dst, k, where):
        pltpu.make_async_remote_copy(
            src_ref=src, dst_ref=dst, send_sem=send_sem.at[k], recv_sem=recv_sem.at[k],
            device_id=where, device_id_type=MESH,
        ).start()

    def local(src, dst, k):
        pltpu.make_async_copy(src, dst, recv_sem.at[k]).start()

    def finish(ref, sem):
        pltpu.make_async_copy(ref, ref, sem).wait()

    for c in range(2):
        for e in peers:
            remote(send.at[2 * e + c], recv.at[c, :, rows_me, :], 1 + c, {"ctx": e})
    for e in peers:
        remote(filt_s, f_dst, 0, {"ctx": e})
    for c in range(2):
        local(send.at[2 * me + c], recv.at[c, :, rows_me, :], 1 + c)
    local(filt_s, f_dst, 0)

    w_row = w_v[...]
    band_a[...] = stack3(jnp.transpose(rolled(w_row, True, N2)))
    band_c[...] = stack3(rolled(w_row, False, N2)[:, :N2])
    alpha = (alpha_s[2 * me], alpha_s[2 * me + 1])
    lam = (lam_s[2 * me], lam_s[2 * me + 1])
    for c in loads[6:]:
        c.wait()
    zw[...] = dot(split3(twist[:N1, :] * jnp.concatenate([w_row, w_row], axis=1)), mix[:768, :])

    for c in range(2):
        finish(recv.at[c], recv_sem.at[1 + c])
        se, so = halves(recv[c, 0])
        ge, go = halves(recv[c, 1])
        forward_exact(
            jnp.concatenate([se, ge], axis=1), jnp.concatenate([so, go], axis=1), fwd, twist, mix, (zs[c], zg[c])
        )
        part = inverse_mix(zg[c], zs[c], twist, mix)
        if c == 0:
            half[0], half[1] = part
    even, odd = inverse_rows([(half[0], half[1]), part], inv)
    re, ro = (even[:, :N2], even[:, N2:]), (odd[:, :N2], odd[:, N2:])
    long_e, long_o, pair = long_rows(re, ro, r_buf, band_a[...], alpha)
    l_rows[pl.ds(0, HALF, 2), :] = long_e
    l_rows[pl.ds(1, HALF, 2), :] = long_o
    l_send[...] = l_rows[...].reshape(128, 4, N2)
    pl.semaphore_wait(ready, len(tp_peers))
    everyone = [(at[o[1:]], tp ^ o[0]) for o in all_offsets()]
    for e, t in everyone:
        remote(l_send.at[n_tp * e + t], l_recv.at[my_id], 5, {"ctx": e, "tp": t})
    local(l_send.at[my_id], l_recv.at[my_id], 5)

    finish(f_buf, recv_sem.at[0])
    fe, fo = f_buf[0], f_buf[1]
    ft_hi, ft_lo = turned_filter(fe, fo)
    s_send[...] = short_row(pair, ft_hi, ft_lo, re, lam)
    for e, t in everyone:
        remote(s_send, s_recv.at[my_id], 6, {"ctx": e, "tp": t})
    local(s_send, s_recv.at[my_id], 6)
    forward_filter(fe, fo, fwd, twist, mix, zf)
    t_hi, t_lo = split(tail_matrix(fo[HALF - 8 :, :], band_c[...]))
    for c in range(2):
        filter_product(zf, zw, lam[c], alpha[c], zv[c])
    even, odd = inverse_rows([inverse_mix(zg[c], zv[c], twist, mix) for c in range(2)], inv)
    for c in range(2):
        s = slice(c * N2, (c + 1) * N2)
        first = recv[c, 1, :16, :]
        fold = (dot(first, t_hi) + dot(first, t_lo))[:1, :]
        last = jnp.concatenate([odd[: HALF - 1, s], odd[HALF - 1 :, s] + fold], axis=0)
        rows = [x.reshape(32, 8, N2) for x in (even[:, s], last)]
        sg_send[c] = jnp.concatenate(rows, axis=1).astype(BF16)
    sg_dst = sg_recv.at[pl.ds(2 * me, 2)]
    for e in peers:
        remote(sg_send.at[:, e], sg_dst, 3, {"ctx": e})
    local(sg_send.at[:, me], sg_dst, 3)

    finish(l_recv, recv_sem.at[5])
    long_out[...] = jnp.sum(l_recv[...], axis=0)
    finish(s_recv, recv_sem.at[6])
    short_out[...] = jnp.sum(s_recv[...], axis=0)
    finish(sg_recv, recv_sem.at[3])
    finish(f_buf.at[:, pl.ds(0, 8 * n_peers), :], send_sem.at[0])
    for c in range(2):
        finish(send.at[pl.ds(0, n_peers)], send_sem.at[1 + c])
    finish(sg_send.at[:, pl.ds(0, n_peers)], send_sem.at[3])
    finish(l_send.at[pl.ds(0, n_all - 1)], send_sem.at[5])
    finish(s_recv.at[pl.ds(0, n_all - 1)], send_sem.at[6])


def lay_out(sg_in, long_in, short_in, sg_out, long_out, short_out, rows, sem):
    swap = swap_matrix(True)
    copies = [
        pltpu.make_async_copy(long_in, long_out, sem.at[2]),
        pltpu.make_async_copy(short_in, short_out, sem.at[3]),
    ]
    for c in copies:
        c.start()
    for g in range(2):
        x = jnp.concatenate(
            [sg_in[32 * g + 16 * h : 32 * g + 16 * (h + 1)].reshape(256, N2) for h in range(2)], axis=1
        )
        y = dot(swap, x).astype(BF16)
        for h in range(2):
            ch = slice(32 * g + 16 * h, 32 * g + 16 * (h + 1))
            for a in range(16):
                rows[ch, N2 * a : N2 * (a + 1)] = y[16 * a : 16 * (a + 1), h * N2 : (h + 1) * N2]
        part = pl.ds(32 * g, 32)
        copies.append(pltpu.make_async_copy(rows.at[part, :], sg_out.at[part, :], sem.at[g]))
        copies[-1].start()
    for c in copies:
        c.wait()


def shards(signal, grad_out, long_filter, short_filter, long_skip, short_skip):
    n_ctx, n_tp = lax.axis_size("ctx"), lax.axis_size("tp")
    consts = [jnp.asarray(t) for t in tables()]
    hbm = pl.BlockSpec(memory_space=pltpu.HBM)
    vmem = pl.BlockSpec(memory_space=pltpu.VMEM)
    V, S = pltpu.VMEM, pltpu.SMEM
    spec = V((N1, 2 * N2), F32)
    raw = pl.pallas_call(
        lambda *refs: kernel(n_ctx, n_tp, *refs),
        out_shape=(
            pltpu.VMEM((64, 16, N2), BF16),
            pltpu.VMEM((4, N2), F32),
            pltpu.VMEM((1, N2), F32),
        ),
        in_specs=[hbm] * 10,
        out_specs=(vmem, vmem, vmem),
        scratch_shapes=[
            V((64, 2048), BF16), V((64, 2048), BF16), V((16, N2), F32), V((2, 8, N2), F32),
            V((1, N2), F32), S((64,), F32), S((64,), F32),
            V((2 * N1, N1), BF16), V((N1, 2 * N1), BF16), V((768, 2 * N2), F32), V((1536, 256), BF16),
            V((64, 2, 16, N2), BF16), V((2, 2, N1, N2), BF16), V((2, HALF, N2), F32),
            spec, spec, spec, spec, spec, spec, spec, V((2, N1, N2), F32), V((HALF + 8, N2), F32),
            V((768, N2), BF16), V((384, N2), BF16), spec,
            V((N1, N2), F32), V((128, 4, N2), F32), V((128, 4, N2), F32), V((1, N2), F32), V((128, 1, N2), F32), V((2, 32, 16, N2), BF16),
            pltpu.SemaphoreType.DMA((10,)), pltpu.SemaphoreType.DMA((7,)), pltpu.SemaphoreType.DMA((7,)),
            pltpu.SemaphoreType.REGULAR,
        ],
        compiler_params=pltpu.CompilerParams(
            collective_id=0, has_side_effects=True, vmem_limit_bytes=60 * 1024 * 1024
        ),
        cost_estimate=pl.CostEstimate(flops=6_000_000_000, bytes_accessed=8_000_000, transcendentals=0),
    )(
        signal, grad_out, long_filter.reshape(16, N2), short_filter.reshape(1, N2),
        long_skip, short_skip, *consts,
    )
    sg, long, short = pl.pallas_call(
        lay_out,
        out_shape=(
            jax.ShapeDtypeStruct((64, 2048), BF16),
            jax.ShapeDtypeStruct((4, N2), F32),
            jax.ShapeDtypeStruct((1, N2), F32),
        ),
        in_specs=[vmem, vmem, vmem],
        out_specs=(hbm, hbm, hbm),
        scratch_shapes=[V((64, 2048), BF16), pltpu.SemaphoreType.DMA((4,))],
    )(*[pltpu.with_memory_space_constraint(r, pltpu.VMEM) for r in raw])
    return sg, long.reshape(512), short.reshape(N2)


def solution(mesh):
    placed = (P("tp", "ctx"), P("tp", "ctx"), P("ctx"), P(), P("tp"), P("tp"))
    return jax.shard_map(
        shards,
        mesh=mesh,
        in_specs=placed,
        out_specs=(P("tp", "ctx"), P(("ctx", "tp")), P()),
        check_vma=False,
    )
```

```python
import math

import jax
import jax.numpy as jnp
import ml_dtypes
import numpy as np
from jax import lax
from jax.experimental import pallas as pl
from jax.experimental.pallas import tpu as pltpu
from jax.sharding import PartitionSpec as P

MESH = pl.DeviceIdType.MESH
F32, BF16 = jnp.float32, jnp.bfloat16
N1, N2 = 512, 128
LEN = N1 * N2
HALF = N1 // 2


def split_np(x):
    x = x.astype(np.float32)
    hi = x.astype(ml_dtypes.bfloat16)
    lo = (x - hi.astype(np.float32)).astype(ml_dtypes.bfloat16)
    return hi, lo


def tables():
    k = np.arange(N1, dtype=np.float64)[:, None] + 0.25
    kh = k[:HALF]
    fwd, inv = [], []
    for odd in range(2):
        n = 2 * np.arange(HALF, dtype=np.float64)[None, :] + odd
        ang = -2 * np.pi * np.mod(kh * n, N1) / N1
        hi, lo = split_np(np.concatenate([np.cos(ang), np.sin(ang)], axis=0))
        fwd.append(np.concatenate([hi, lo], axis=1))
        inv.append(np.concatenate([hi.T, lo.T], axis=1))
    m = np.arange(N2, dtype=np.float64)
    ang = -2 * np.pi * k * m[None, :] / LEN
    twist = np.concatenate([np.cos(ang), np.sin(ang)], axis=1)
    ang = np.broadcast_to(-2 * np.pi * kh / N1, (HALF, N2))
    twist = np.concatenate([twist, np.concatenate([np.cos(ang), np.sin(ang)], axis=1)]).astype(np.float32)
    ang = -2 * np.pi * np.mod(m[:, None] * m[None, :], N2) / N2
    br, bi = np.cos(ang), np.sin(ang)
    b_hi, b_lo = split_np(np.block([[br, bi], [-bi, br]]))
    c_hi, c_lo = split_np(np.block([[br, -bi], [bi, br]]) / LEN)
    mix = np.concatenate([b_hi, b_hi, b_lo, c_hi, c_hi, c_lo])
    return np.concatenate(fwd), np.concatenate(inv), twist, mix


def dot(a, b):
    return jnp.dot(a, b, preferred_element_type=F32)


def split(x):
    hi = x.astype(BF16)
    return hi, (x - hi.astype(F32)).astype(BF16)


def split3(x):
    hi, lo = split(x)
    return jnp.concatenate([hi, lo, hi], axis=1)


def twice(x):
    return jnp.concatenate([x, x], axis=0)


def mix_forward(even, odd, twist, mix, z_refs):
    for q, z in enumerate(z_refs):
        s = slice(q * N2, (q + 1) * N2)
        er, ei, dr, di = even[:HALF, s], even[HALF:, s], odd[:HALF, s], odd[HALF:, s]
        for h, (xr, xi) in enumerate([(er + dr, ei + di), (er - dr, ei - di)]):
            r = slice(h * HALF, (h + 1) * HALF)
            tr, ti = twist[r, :N2], twist[r, N2:]
            y = jnp.concatenate([xr * tr - xi * ti, xi * tr + xr * ti], axis=1)
            z[r, :] = dot(split3(y), mix[:768, :])


def forward_exact(xe, xo, fwd, twist, mix, z_refs):
    mix_forward(dot(fwd[:N1, :], twice(xe)), dot(fwd[N1:, :], twice(xo)), twist, mix, z_refs)


def forward_filter(fe, fo, fwd, twist, mix, z):
    hi, lo = split(jnp.concatenate([fe, fo], axis=1))
    yr, yi = (dot(fwd[r, :], twice(hi)) + dot(fwd[r, :HALF], lo) for r in (slice(0, HALF), slice(HALF, N1)))
    tr, ti = twist[N1:, :N2], twist[N1:, N2:]
    dr, di = yr[:, N2:], yi[:, N2:]
    even = jnp.concatenate([yr[:, :N2], yi[:, :N2]], axis=0)
    odd = jnp.concatenate([dr * tr - di * ti, di * tr + dr * ti], axis=0)
    mix_forward(even, odd, twist, mix, (z,))


def inverse_mix(a, b, twist, mix):
    ys = []
    for h in range(2):
        r = slice(h * HALF, (h + 1) * HALF)
        ar, ai, br, bi = a[r, :N2], a[r, N2:], b[r, :N2], b[r, N2:]
        z = jnp.concatenate([ar * br + ai * bi, ai * br - ar * bi], axis=1)
        y = dot(split3(z), mix[768:, :])
        yr, yi = y[:, :N2], y[:, N2:]
        tr, ti = twist[r, :N2], twist[r, N2:]
        ys.append(jnp.concatenate([yr * tr + yi * ti, yi * tr - yr * ti], axis=0))
    return ys[0] + ys[1], ys[0] - ys[1]


def inverse_rows(halves, inv):
    out = []
    for h in range(2):
        hi, lo = split(jnp.concatenate([x[h] for x in halves], axis=1))
        r = slice(h * HALF, (h + 1) * HALF)
        out.append(dot(inv[r, :], twice(hi)) + dot(inv[r, :N1], lo))
    return out


def one_hot(cond):
    return jnp.where(cond, 1.0, 0.0).astype(BF16)


def swap_matrix(back):
    i = lax.broadcasted_iota(jnp.int32, (256, 256), 0)
    j = lax.broadcasted_iota(jnp.int32, (256, 256), 1)
    if back:
        i, j = j, i
    p = i % 16
    return one_hot((i // 16 == j % 16) & (2 * (p % 8) + p // 8 == j // 16))


def rolled(w_row, first, rows):
    zero = jnp.zeros((1, N2), F32)
    base = jnp.concatenate([w_row, zero] if first else [zero, w_row], axis=1)
    return pltpu.roll(jnp.broadcast_to(base, (rows, 2 * N2)), 0, 1, stride=1, stride_axis=0)


def stack3(x):
    hi, lo = split(x)
    return jnp.concatenate([hi, hi, lo], axis=0)


def long_rows(re, ro, r_buf, band, alpha):
    se, so = re[0] + re[1], ro[0] + ro[1]
    r_buf[:HALF, :] = se
    pair = jnp.concatenate(
        [jnp.concatenate([se, so], axis=1), jnp.concatenate([so, r_buf[pl.ds(1, HALF), :]], axis=1)], axis=0
    )
    long = dot(split3(pair), band)
    long_e = long[:HALF] + (alpha[0] * re[0] + alpha[1] * re[1])
    long_o = long[HALF:] + (alpha[0] * ro[0] + alpha[1] * ro[1])
    return long_e, long_o, pair


def turned_filter(fe, fo):
    i = lax.broadcasted_iota(jnp.int32, (N2, N2), 0)
    j = lax.broadcasted_iota(jnp.int32, (N2, N2), 1)
    flip = one_hot(i + j == N2 - 1)
    hi, lo = split(jnp.transpose(jnp.concatenate([fe, fo], axis=0)))
    return dot(flip, hi).astype(BF16), dot(flip, lo).astype(BF16)


def short_row(pair, f_hi, f_lo, re, lam):
    hi, lo = split(pair)
    cross = dot(f_hi, hi) + (dot(f_hi, lo) + dot(f_lo, hi))
    diag = pltpu.roll(cross, N2 + 1, 1, stride=1, stride_axis=0)
    short = jnp.sum(diag, axis=0, keepdims=True)[:, :N2]
    return short + (lam[0] * re[0][:1, :] + lam[1] * re[1][:1, :])


def filter_product(zf, zw, lam, alpha, zv):
    fr, fi = zf[:, :N2] + lam, zf[:, N2:]
    wr, wi = zw[:, :N2] + alpha, zw[:, N2:]
    zv[:, :N2] = fr * wr - fi * wi
    zv[:, N2:] = fr * wi + fi * wr


def tail_matrix(f_last, band):
    tail = dot(split3(f_last), band)
    i = lax.broadcasted_iota(jnp.int32, (N2, N2), 0)
    j = lax.broadcasted_iota(jnp.int32, (N2, N2), 1)
    flip = one_hot(i + j == N2)
    hi, lo = split(tail)
    turned = (dot(hi, flip) + dot(lo, flip))[7:, :]
    return rolled(turned, True, N2)[:, :N2]


def halves(x):
    x = x.astype(F32)
    return x[:, :8].reshape(HALF, N2).astype(BF16), x[:, 8:].reshape(HALF, N2).astype(BF16)


def offsets():
    def far(o):
        return o[0] + min(o[1], 4 - o[1]) + min(o[2], 4 - o[2])

    out = [(y, z, x) for y in range(2) for z in range(4) for x in range(4)][1:]
    return sorted(out, key=lambda o: -far(o))


def all_offsets():
    def far(o):
        y = (1 if o[1] else 2) if o[0] & 2 else o[1]
        return y + min(o[2], 4 - o[2]) + min(o[3], 4 - o[3])

    out = [(t, y, z, x) for y in range(2) for z in range(4) for x in range(4) for t in range(4)][1:]
    return sorted(out, key=lambda o: -far(o))


def kernel(
    n_ctx, n_tp,
    sig, cot, filt, w_in, lam_in, alpha_in, f_tab, i_tab, t_tab, m_tab,
    sg_recv, long_out, short_out,
    sig_v, cot_v, filt_v, filt_s, w_v, lam_s, alpha_s, fwd, inv, twist, mix,
    send, recv, f_buf, zs0, zg0, zs1, zg1, zf, zv0, zv1, half, r_buf, band_a, band_c, zw,
    l_send, l_recv, s_send, s_recv, sg_send, load_sem, send_sem, recv_sem, ready,
):
    me, tp = lax.axis_index("ctx"), lax.axis_index("tp")
    zs, zg, zv = (zs0, zs1), (zg0, zg1), (zv0, zv1)
    my_y, my_z, my_x = me // 16, (me // 4) % 4, me % 4
    at = {(y, z, x): (my_y ^ y) * 16 + ((my_z + z) & 3) * 4 + ((my_x + x) & 3) for y, z, x in [(0, 0, 0)] + offsets()}
    peers = [at[o] for o in offsets()]
    tp_peers = [tp ^ i for i in (3, 2, 1)]
    n_peers = len(peers)
    n_all = n_ctx * n_tp
    my_id = n_tp * me + tp

    barrier = pltpu.get_barrier_semaphore()
    for e in peers:
        pl.semaphore_signal(barrier, inc=1, device_id={"ctx": e}, device_id_type=MESH)
    for t in tp_peers:
        pl.semaphore_signal(barrier, inc=1, device_id={"tp": t}, device_id_type=MESH)
    loads = [
        pltpu.make_async_copy(src, dst, load_sem.at[i])
        for i, (src, dst) in enumerate(
            [(filt, filt_v), (sig, sig_v), (cot, cot_v), (w_in, w_v), (lam_in, lam_s), (alpha_in, alpha_s),
             (f_tab, fwd), (t_tab, twist), (m_tab, mix), (i_tab, inv)]
        )
    ]
    for c in loads:
        c.start()
    r_buf[HALF:, :] = jnp.zeros((8, N2), F32)
    swap = swap_matrix(False)
    for c in loads[:6]:
        c.wait()
    for h in range(2):
        for i in range(8):
            filt_s[h, i : i + 1, :] = filt_v[2 * i + h : 2 * i + h + 1, :]
    for g in range(4):
        ch = slice(16 * g, 16 * (g + 1))
        x = jnp.concatenate(
            [
                jnp.concatenate([v[ch, N2 * a : N2 * (a + 1)] for a in range(16)], axis=0)
                for v in (sig_v, cot_v)
            ],
            axis=1,
        )
        y = dot(swap, x).astype(BF16)
        send[ch, 0] = y[:, :N2].reshape(16, 16, N2)
        send[ch, 1] = y[:, N2:].reshape(16, 16, N2)
    pl.semaphore_wait(barrier, n_peers + len(tp_peers))
    for t in tp_peers:
        pl.semaphore_signal(ready, inc=1, device_id={"tp": t}, device_id_type=MESH)

    f_dst = f_buf.at[me]

    def remote(src, dst, k, where):
        pltpu.make_async_remote_copy(
            src_ref=src, dst_ref=dst, send_sem=send_sem.at[k], recv_sem=recv_sem.at[k],
            device_id=where, device_id_type=MESH,
        ).start()

    def local(src, dst, k):
        pltpu.make_async_copy(src, dst, recv_sem.at[k]).start()

    def finish(ref, sem):
        pltpu.make_async_copy(ref, ref, sem).wait()

    for c in range(2):
        for e in peers:
            remote(send.at[2 * e + c], recv.at[c, me], 1 + c, {"ctx": e})
    for e in peers:
        remote(filt_s, f_dst, 0, {"ctx": e})
    for c in range(2):
        local(send.at[2 * me + c], recv.at[c, me], 1 + c)
    local(filt_s, f_dst, 0)

    w_row = w_v[...]
    band_a[...] = stack3(jnp.transpose(rolled(w_row, True, N2)))
    band_c[...] = stack3(rolled(w_row, False, N2)[:, :N2])
    alpha = (alpha_s[2 * me], alpha_s[2 * me + 1])
    lam = (lam_s[2 * me], lam_s[2 * me + 1])
    for c in loads[6:]:
        c.wait()
    zw[...] = dot(split3(twist[:N1, :] * jnp.concatenate([w_row, w_row], axis=1)), mix[:768, :])

    for c in range(2):
        finish(recv.at[c], recv_sem.at[1 + c])
        se, so = halves(recv[c, :, 0])
        ge, go = halves(recv[c, :, 1])
        forward_exact(
            jnp.concatenate([se, ge], axis=1), jnp.concatenate([so, go], axis=1), fwd, twist, mix, (zs[c], zg[c])
        )
        part = inverse_mix(zg[c], zs[c], twist, mix)
        if c == 0:
            half[0], half[1] = part
    even, odd = inverse_rows([(half[0], half[1]), part], inv)
    re, ro = (even[:, :N2], even[:, N2:]), (odd[:, :N2], odd[:, N2:])
    long_e, long_o, pair = long_rows(re, ro, r_buf, band_a[...], alpha)
    l_send[pl.ds(0, HALF, 2), :] = long_e
    l_send[pl.ds(1, HALF, 2), :] = long_o
    pl.semaphore_wait(ready, len(tp_peers))
    everyone = [(at[o[1:]], tp ^ o[0]) for o in all_offsets()]
    l_dst = l_recv.at[pl.ds(pl.multiple_of(4 * my_id, 4), 4), :]
    for e, t in everyone:
        src = l_send.at[pl.ds(pl.multiple_of(4 * (n_tp * e + t), 4), 4), :]
        remote(src, l_dst, 5, {"ctx": e, "tp": t})
    local(l_send.at[pl.ds(pl.multiple_of(4 * my_id, 4), 4), :], l_dst, 5)

    finish(f_buf, recv_sem.at[0])
    fe, fo = f_buf[:, 0].reshape(HALF, N2), f_buf[:, 1].reshape(HALF, N2)
    ft_hi, ft_lo = turned_filter(fe, fo)
    s_send[...] = short_row(pair, ft_hi, ft_lo, re, lam)
    for e, t in everyone:
        remote(s_send, s_recv.at[my_id], 6, {"ctx": e, "tp": t})
    local(s_send, s_recv.at[my_id], 6)
    forward_filter(fe, fo, fwd, twist, mix, zf)
    t_hi, t_lo = split(tail_matrix(fo[HALF - 8 :, :], band_c[...]))
    for c in range(2):
        filter_product(zf, zw, lam[c], alpha[c], zv[c])
    halves_sg = [inverse_mix(zg[c], zv[c], twist, mix) for c in range(2)]
    sg_dst = sg_recv.at[pl.ds(2 * me, 2)]
    folds = [(dot(recv[c, 0, 1], t_hi) + dot(recv[c, 0, 1], t_lo))[:1, :] for c in range(2)]
    ys = [split(jnp.concatenate([x[h] for x in halves_sg], axis=1)) for h in range(2)]
    for p in range(2):
        even, odd = (
            dot(inv[r, :], twice(hi)) + dot(inv[r, :N1], lo)
            for (hi, lo), r in zip(ys, (slice(h * HALF + 128 * p, h * HALF + 128 * (p + 1)) for h in range(2)))
        )
        for c in range(2):
            s = slice(c * N2, (c + 1) * N2)
            last = odd[:, s]
            if p == 1:
                last = jnp.concatenate([last[:127], last[127:] + folds[c]], axis=0)
            rows = [x.reshape(16, 8, N2) for x in (even[:, s], last)]
            sg_send[16 * p : 16 * (p + 1), c] = jnp.concatenate(rows, axis=1).astype(BF16)
        for z in (2, 1, 3, 0):
            for x in (2, 1, 3, 0):
                e = 16 * p + ((my_z + z) & 3) * 4 + ((my_x + x) & 3)
                if z or x:
                    remote(sg_send.at[e], sg_dst, 3, {"ctx": e})
                else:

                    @pl.when(my_y != p)
                    def _():
                        remote(sg_send.at[e], sg_dst, 3, {"ctx": e})

    local(sg_send.at[me], sg_dst, 3)

    finish(l_recv, recv_sem.at[5])
    total = jnp.sum(l_recv[...].reshape(64, 8, N2), axis=0)
    long_out[...] = total[:4] + total[4:]
    finish(s_recv, recv_sem.at[6])
    short_out[...] = jnp.sum(s_recv[...], axis=0)
    finish(sg_recv, recv_sem.at[3])
    finish(f_buf.at[pl.ds(0, n_peers)], send_sem.at[0])
    for c in range(2):
        finish(send.at[pl.ds(0, n_peers)], send_sem.at[1 + c])
    finish(sg_send.at[pl.ds(0, n_peers)], send_sem.at[3])
    finish(l_send.at[pl.ds(0, 4 * (n_all - 1)), :], send_sem.at[5])
    finish(s_recv.at[pl.ds(0, n_all - 1)], send_sem.at[6])


def lay_out(sg_in, long_in, short_in, sg_out, long_out, short_out, rows, sem):
    swap = swap_matrix(True)
    copies = [
        pltpu.make_async_copy(long_in, long_out, sem.at[2]),
        pltpu.make_async_copy(short_in, short_out, sem.at[3]),
    ]
    for c in copies:
        c.start()
    for g in range(2):
        x = jnp.concatenate(
            [sg_in[32 * g + 16 * h : 32 * g + 16 * (h + 1)].reshape(256, N2) for h in range(2)], axis=1
        )
        y = dot(swap, x).astype(BF16)
        for h in range(2):
            ch = slice(32 * g + 16 * h, 32 * g + 16 * (h + 1))
            for a in range(16):
                rows[ch, N2 * a : N2 * (a + 1)] = y[16 * a : 16 * (a + 1), h * N2 : (h + 1) * N2]
        part = pl.ds(32 * g, 32)
        copies.append(pltpu.make_async_copy(rows.at[part, :], sg_out.at[part, :], sem.at[g]))
        copies[-1].start()
    for c in copies:
        c.wait()


def shards(signal, grad_out, long_filter, short_filter, long_skip, short_skip):
    n_ctx, n_tp = lax.axis_size("ctx"), lax.axis_size("tp")
    consts = [jnp.asarray(t) for t in tables()]
    hbm = pl.BlockSpec(memory_space=pltpu.HBM)
    vmem = pl.BlockSpec(memory_space=pltpu.VMEM)
    V, S = pltpu.VMEM, pltpu.SMEM
    spec = V((N1, 2 * N2), F32)
    raw = pl.pallas_call(
        lambda *refs: kernel(n_ctx, n_tp, *refs),
        out_shape=(
            pltpu.VMEM((64, 16, N2), BF16),
            pltpu.VMEM((4, N2), F32),
            pltpu.VMEM((1, N2), F32),
        ),
        in_specs=[hbm] * 10,
        out_specs=(vmem, vmem, vmem),
        scratch_shapes=[
            V((64, 2048), BF16), V((64, 2048), BF16), V((16, N2), F32), V((2, 8, N2), F32),
            V((1, N2), F32), S((64,), F32), S((64,), F32),
            V((2 * N1, N1), BF16), V((N1, 2 * N1), BF16), V((768, 2 * N2), F32), V((1536, 256), BF16),
            V((64, 2, 16, N2), BF16), V((2, 32, 2, 16, N2), BF16), V((32, 2, 8, N2), F32),
            spec, spec, spec, spec, spec, spec, spec, V((2, N1, N2), F32), V((HALF + 8, N2), F32),
            V((768, N2), BF16), V((384, N2), BF16), spec,
            V((N1, N2), F32), V((N1, N2), F32), V((1, N2), F32), V((128, 1, N2), F32), V((32, 2, 16, N2), BF16),
            pltpu.SemaphoreType.DMA((10,)), pltpu.SemaphoreType.DMA((7,)), pltpu.SemaphoreType.DMA((7,)),
            pltpu.SemaphoreType.REGULAR,
        ],
        compiler_params=pltpu.CompilerParams(
            collective_id=0, has_side_effects=True, vmem_limit_bytes=60 * 1024 * 1024
        ),
        cost_estimate=pl.CostEstimate(flops=6_000_000_000, bytes_accessed=8_000_000, transcendentals=0),
    )(
        signal, grad_out, long_filter.reshape(16, N2), short_filter.reshape(1, N2),
        long_skip, short_skip, *consts,
    )
    sg, long, short = pl.pallas_call(
        lay_out,
        out_shape=(
            jax.ShapeDtypeStruct((64, 2048), BF16),
            jax.ShapeDtypeStruct((4, N2), F32),
            jax.ShapeDtypeStruct((1, N2), F32),
        ),
        in_specs=[vmem, vmem, vmem],
        out_specs=(hbm, hbm, hbm),
        scratch_shapes=[V((64, 2048), BF16), pltpu.SemaphoreType.DMA((4,))],
    )(*[pltpu.with_memory_space_constraint(r, pltpu.VMEM) for r in raw])
    return sg, long.reshape(512), short.reshape(N2)


def solution(mesh):
    placed = (P("tp", "ctx"), P("tp", "ctx"), P("ctx"), P(), P("tp"), P("tp"))
    return jax.shard_map(
        shards,
        mesh=mesh,
        in_specs=placed,
        out_specs=(P("tp", "ctx"), P(("ctx", "tp")), P()),
        check_vma=False,
    )
```

```python
import math

import jax
import jax.numpy as jnp
import ml_dtypes
import numpy as np
from jax import lax
from jax.experimental import pallas as pl
from jax.experimental.pallas import tpu as pltpu
from jax.sharding import PartitionSpec as P

MESH = pl.DeviceIdType.MESH
F32, BF16 = jnp.float32, jnp.bfloat16
N1, N2 = 512, 128
LEN = N1 * N2
HALF = N1 // 2


def split_np(x):
    x = x.astype(np.float32)
    hi = x.astype(ml_dtypes.bfloat16)
    lo = (x - hi.astype(np.float32)).astype(ml_dtypes.bfloat16)
    return hi, lo


def tables():
    k = np.arange(N1, dtype=np.float64)[:, None] + 0.25
    kh = k[:HALF]
    fwd, inv = [], []
    for odd in range(2):
        n = 2 * np.arange(HALF, dtype=np.float64)[None, :] + odd
        ang = -2 * np.pi * np.mod(kh * n, N1) / N1
        hi, lo = split_np(np.concatenate([np.cos(ang), np.sin(ang)], axis=0))
        fwd.append(np.concatenate([hi, lo], axis=1))
        inv.append(np.concatenate([hi.T, lo.T], axis=1))
    m = np.arange(N2, dtype=np.float64)
    ang = -2 * np.pi * k * m[None, :] / LEN
    twist = np.concatenate([np.cos(ang), np.sin(ang)], axis=1)
    ang = np.broadcast_to(-2 * np.pi * kh / N1, (HALF, N2))
    twist = np.concatenate([twist, np.concatenate([np.cos(ang), np.sin(ang)], axis=1)]).astype(np.float32)
    ang = -2 * np.pi * np.mod(m[:, None] * m[None, :], N2) / N2
    br, bi = np.cos(ang), np.sin(ang)
    b_hi, b_lo = split_np(np.block([[br, bi], [-bi, br]]))
    c_hi, c_lo = split_np(np.block([[br, -bi], [bi, br]]) / LEN)
    mix = np.concatenate([b_hi, b_hi, b_lo, c_hi, c_hi, c_lo])
    return np.concatenate(fwd), np.concatenate(inv), twist, mix


def dot(a, b):
    return jnp.dot(a, b, preferred_element_type=F32)


def split(x):
    hi = x.astype(BF16)
    return hi, (x - hi.astype(F32)).astype(BF16)


def split3(x):
    hi, lo = split(x)
    return jnp.concatenate([hi, lo, hi], axis=1)


def twice(x):
    return jnp.concatenate([x, x], axis=0)


def mix_forward(even, odd, twist, mix, z_refs):
    for q, z in enumerate(z_refs):
        s = slice(q * N2, (q + 1) * N2)
        er, ei, dr, di = even[:HALF, s], even[HALF:, s], odd[:HALF, s], odd[HALF:, s]
        for h, (xr, xi) in enumerate([(er + dr, ei + di), (er - dr, ei - di)]):
            r = slice(h * HALF, (h + 1) * HALF)
            tr, ti = twist[r, :N2], twist[r, N2:]
            y = jnp.concatenate([xr * tr - xi * ti, xi * tr + xr * ti], axis=1)
            z[r, :] = dot(split3(y), mix[:768, :])


def forward_exact(xe, xo, fwd, twist, mix, z_refs):
    mix_forward(dot(fwd[:N1, :], twice(xe)), dot(fwd[N1:, :], twice(xo)), twist, mix, z_refs)


def forward_filter(fe, fo, fwd, twist, mix, z):
    hi, lo = split(jnp.concatenate([fe, fo], axis=1))
    yr, yi = (dot(fwd[r, :], twice(hi)) + dot(fwd[r, :HALF], lo) for r in (slice(0, HALF), slice(HALF, N1)))
    tr, ti = twist[N1:, :N2], twist[N1:, N2:]
    dr, di = yr[:, N2:], yi[:, N2:]
    even = jnp.concatenate([yr[:, :N2], yi[:, :N2]], axis=0)
    odd = jnp.concatenate([dr * tr - di * ti, di * tr + dr * ti], axis=0)
    mix_forward(even, odd, twist, mix, (z,))


def inverse_mix(a, b, twist, mix):
    ys = []
    for h in range(2):
        r = slice(h * HALF, (h + 1) * HALF)
        ar, ai, br, bi = a[r, :N2], a[r, N2:], b[r, :N2], b[r, N2:]
        z = jnp.concatenate([ar * br + ai * bi, ai * br - ar * bi], axis=1)
        y = dot(split3(z), mix[768:, :])
        yr, yi = y[:, :N2], y[:, N2:]
        tr, ti = twist[r, :N2], twist[r, N2:]
        ys.append(jnp.concatenate([yr * tr + yi * ti, yi * tr - yr * ti], axis=0))
    return ys[0] + ys[1], ys[0] - ys[1]


def inverse_rows(halves, inv):
    out = []
    for h in range(2):
        hi, lo = split(jnp.concatenate([x[h] for x in halves], axis=1))
        r = slice(h * HALF, (h + 1) * HALF)
        out.append(dot(inv[r, :], twice(hi)) + dot(inv[r, :N1], lo))
    return out


def one_hot(cond):
    return jnp.where(cond, 1.0, 0.0).astype(BF16)


def swap_matrix(back):
    i = lax.broadcasted_iota(jnp.int32, (256, 256), 0)
    j = lax.broadcasted_iota(jnp.int32, (256, 256), 1)
    if back:
        i, j = j, i
    p = i & 15
    return one_hot(((i >> 4) == (j & 15)) & (2 * (p & 7) + (p >> 3) == (j >> 4)))


def rolled(w_row, first, rows):
    zero = jnp.zeros((1, N2), F32)
    base = jnp.concatenate([w_row, zero] if first else [zero, w_row], axis=1)
    return pltpu.roll(jnp.broadcast_to(base, (rows, 2 * N2)), 0, 1, stride=1, stride_axis=0)


def stack3(x):
    hi, lo = split(x)
    return jnp.concatenate([hi, hi, lo], axis=0)


def long_rows(re, ro, r_buf, band, alpha):
    se, so = re[0] + re[1], ro[0] + ro[1]
    r_buf[:HALF, :] = se
    pair = jnp.concatenate(
        [jnp.concatenate([se, so], axis=1), jnp.concatenate([so, r_buf[pl.ds(1, HALF), :]], axis=1)], axis=0
    )
    long = dot(split3(pair), band)
    long_e = long[:HALF] + (alpha[0] * re[0] + alpha[1] * re[1])
    long_o = long[HALF:] + (alpha[0] * ro[0] + alpha[1] * ro[1])
    return long_e, long_o, pair


def turned_filter(fe, fo):
    i = lax.broadcasted_iota(jnp.int32, (N2, N2), 0)
    j = lax.broadcasted_iota(jnp.int32, (N2, N2), 1)
    flip = one_hot(i + j == N2 - 1)
    hi, lo = split(jnp.transpose(jnp.concatenate([fe, fo], axis=0)))
    return dot(flip, hi).astype(BF16), dot(flip, lo).astype(BF16)


def short_row(pair, f_hi, f_lo, re, lam):
    hi, lo = split(pair)
    cross = dot(f_hi, hi) + (dot(f_hi, lo) + dot(f_lo, hi))
    diag = pltpu.roll(cross, N2 + 1, 1, stride=1, stride_axis=0)
    short = jnp.sum(diag, axis=0, keepdims=True)[:, :N2]
    return short + (lam[0] * re[0][:1, :] + lam[1] * re[1][:1, :])


def filter_product(zf, zw, lam, alpha, zv):
    fr, fi = zf[:, :N2] + lam, zf[:, N2:]
    wr, wi = zw[:, :N2] + alpha, zw[:, N2:]
    zv[:, :N2] = fr * wr - fi * wi
    zv[:, N2:] = fr * wi + fi * wr


def tail_matrix(f_last, band):
    tail = dot(split3(f_last), band)
    i = lax.broadcasted_iota(jnp.int32, (N2, N2), 0)
    j = lax.broadcasted_iota(jnp.int32, (N2, N2), 1)
    flip = one_hot(i + j == N2)
    hi, lo = split(tail)
    turned = (dot(hi, flip) + dot(lo, flip))[7:, :]
    return rolled(turned, True, N2)[:, :N2]


def halves(x):
    x = x.astype(F32)
    return x[:, :8].reshape(HALF, N2).astype(BF16), x[:, 8:].reshape(HALF, N2).astype(BF16)


def offsets():
    def far(o):
        return o[0] + min(o[1], 4 - o[1]) + min(o[2], 4 - o[2])

    out = [(y, z, x) for y in range(2) for z in range(4) for x in range(4)][1:]
    return sorted(out, key=lambda o: -far(o))


def all_offsets():
    def far(o):
        y = (1 if o[1] else 2) if o[0] & 2 else o[1]
        return y + min(o[2], 4 - o[2]) + min(o[3], 4 - o[3])

    out = [(t, y, z, x) for y in range(2) for z in range(4) for x in range(4) for t in range(4)][1:]
    return sorted(out, key=lambda o: (-(o[0] & 2), -far(o)))


def kernel(
    n_ctx, n_tp,
    sig, cot, filt, w_in, lam_in, alpha_in, f_tab, i_tab, t_tab, m_tab,
    sg_recv, long_out, short_out, swap_out,
    sig_v, cot_v, filt_v, filt_s, w_v, lam_s, alpha_s, fwd, inv, twist, mix,
    send, recv, f_buf, zs0, zg0, zs1, zg1, zf, zv0, zv1, half, r_buf, band_a, band_c, zw,
    l_send, l_recv, s_send, s_recv, sg_send, load_sem, send_sem, recv_sem, ready,
):
    me, tp = lax.axis_index("ctx"), lax.axis_index("tp")
    zs, zg, zv = (zs0, zs1), (zg0, zg1), (zv0, zv1)
    my_y, my_z, my_x = me // 16, (me // 4) % 4, me % 4
    at = {(y, z, x): (my_y ^ y) * 16 + ((my_z + z) & 3) * 4 + ((my_x + x) & 3) for y, z, x in [(0, 0, 0)] + offsets()}
    peers = [at[o] for o in offsets()]
    tp_peers = [tp ^ i for i in (3, 2, 1)]
    n_peers = len(peers)
    n_all = n_ctx * n_tp
    my_id = n_tp * me + tp

    barrier = pltpu.get_barrier_semaphore()
    for e in peers:
        pl.semaphore_signal(barrier, inc=1, device_id={"ctx": e}, device_id_type=MESH)
    for t in tp_peers:
        pl.semaphore_signal(barrier, inc=1, device_id={"tp": t}, device_id_type=MESH)
    loads = [
        pltpu.make_async_copy(src, dst, load_sem.at[i])
        for i, (src, dst) in enumerate(
            [(filt, filt_v), (sig, sig_v), (cot, cot_v), (w_in, w_v), (lam_in, lam_s), (alpha_in, alpha_s),
             (f_tab, fwd), (t_tab, twist), (m_tab, mix), (i_tab, inv)]
        )
    ]
    for c in loads:
        c.start()
    r_buf[HALF:, :] = jnp.zeros((8, N2), F32)
    swap = swap_matrix(False)
    for c in loads[:6]:
        c.wait()
    for h in range(2):
        for i in range(8):
            filt_s[h, i : i + 1, :] = filt_v[2 * i + h : 2 * i + h + 1, :]
    for g in range(4):
        ch = slice(16 * g, 16 * (g + 1))
        x = jnp.concatenate(
            [
                jnp.concatenate([v[ch, N2 * a : N2 * (a + 1)] for a in range(16)], axis=0)
                for v in (sig_v, cot_v)
            ],
            axis=1,
        )
        y = dot(swap, x).astype(BF16)
        send[ch, 0] = y[:, :N2].reshape(16, 16, N2)
        send[ch, 1] = y[:, N2:].reshape(16, 16, N2)
    pl.semaphore_wait(barrier, n_peers + len(tp_peers))

    f_dst = f_buf.at[me]

    def remote(src, dst, k, where):
        pltpu.make_async_remote_copy(
            src_ref=src, dst_ref=dst, send_sem=send_sem.at[k], recv_sem=recv_sem.at[k],
            device_id=where, device_id_type=MESH,
        ).start()

    def local(src, dst, k):
        pltpu.make_async_copy(src, dst, recv_sem.at[k]).start()

    def finish(ref, sem):
        pltpu.make_async_copy(ref, ref, sem).wait()

    for e in peers:
        remote(send.at[2 * e], recv.at[0, me], 1, {"ctx": e})
    for q in range(2):
        for e in peers:
            remote(send.at[2 * e + 1, q], recv.at[1, me, q], 2 + 5 * q, {"ctx": e})
    for e in peers:
        remote(filt_s, f_dst, 0, {"ctx": e})
    local(send.at[2 * me], recv.at[0, me], 1)
    for q in range(2):
        local(send.at[2 * me + 1, q], recv.at[1, me, q], 2 + 5 * q)
    local(filt_s, f_dst, 0)

    for t in tp_peers:
        pl.semaphore_signal(ready, inc=1, device_id={"tp": t}, device_id_type=MESH)
    swap_out[...] = swap_matrix(True)
    w_row = w_v[...]
    band_a[...] = stack3(jnp.transpose(rolled(w_row, True, N2)))
    band_c[...] = stack3(rolled(w_row, False, N2)[:, :N2])
    alpha = (alpha_s[2 * me], alpha_s[2 * me + 1])
    lam = (lam_s[2 * me], lam_s[2 * me + 1])
    for c in loads[6:]:
        c.wait()
    zw[...] = dot(split3(twist[:N1, :] * jnp.concatenate([w_row, w_row], axis=1)), mix[:768, :])

    finish(recv.at[0], recv_sem.at[1])
    se, so = halves(recv[0, :, 0])
    ge, go = halves(recv[0, :, 1])
    forward_exact(jnp.concatenate([se, ge], axis=1), jnp.concatenate([so, go], axis=1), fwd, twist, mix, (zs0, zg0))
    half[0], half[1] = inverse_mix(zg0, zs0, twist, mix)
    for q, z in enumerate((zs1, zg1)):
        finish(recv.at[1, :, q], recv_sem.at[2 + 5 * q])
        xe, xo = halves(recv[1, :, q])
        forward_exact(xe, xo, fwd, twist, mix, (z,))
    part = inverse_mix(zg1, zs1, twist, mix)
    even, odd = inverse_rows([(half[0], half[1]), part], inv)
    re, ro = (even[:, :N2], even[:, N2:]), (odd[:, :N2], odd[:, N2:])
    long_e, long_o, pair = long_rows(re, ro, r_buf, band_a[...], alpha)
    l_send[pl.ds(0, HALF, 2), :] = long_e
    l_send[pl.ds(1, HALF, 2), :] = long_o
    pl.semaphore_wait(ready, len(tp_peers))
    everyone = [(at[o[1:]], tp ^ o[0]) for o in all_offsets()]
    l_dst = l_recv.at[pl.ds(pl.multiple_of(4 * my_id, 4), 4), :]
    for e, t in everyone:
        src = l_send.at[pl.ds(pl.multiple_of(4 * (n_tp * e + t), 4), 4), :]
        remote(src, l_dst, 5, {"ctx": e, "tp": t})
    local(l_send.at[pl.ds(pl.multiple_of(4 * my_id, 4), 4), :], l_dst, 5)

    finish(f_buf, recv_sem.at[0])
    fe, fo = f_buf[:, 0].reshape(HALF, N2), f_buf[:, 1].reshape(HALF, N2)
    ft_hi, ft_lo = turned_filter(fe, fo)
    s_send[...] = short_row(pair, ft_hi, ft_lo, re, lam)
    for e, t in everyone:
        remote(s_send, s_recv.at[my_id], 6, {"ctx": e, "tp": t})
    local(s_send, s_recv.at[my_id], 6)
    forward_filter(fe, fo, fwd, twist, mix, zf)
    t_hi, t_lo = split(tail_matrix(fo[HALF - 8 :, :], band_c[...]))
    for c in range(2):
        filter_product(zf, zw, lam[c], alpha[c], zv[c])
    halves_sg = [inverse_mix(zg[c], zv[c], twist, mix) for c in range(2)]
    sg_dst = sg_recv.at[pl.ds(2 * me, 2)]
    folds = [(dot(recv[c, 0, 1], t_hi) + dot(recv[c, 0, 1], t_lo))[:1, :] for c in range(2)]
    ys = [split(jnp.concatenate([x[h] for x in halves_sg], axis=1)) for h in range(2)]
    for p in range(2):
        even, odd = (
            dot(inv[r, :], twice(hi)) + dot(inv[r, :N1], lo)
            for (hi, lo), r in zip(ys, (slice(h * HALF + 128 * p, h * HALF + 128 * (p + 1)) for h in range(2)))
        )
        for c in range(2):
            s = slice(c * N2, (c + 1) * N2)
            last = odd[:, s]
            if p == 1:
                last = jnp.concatenate([last[:127], last[127:] + folds[c]], axis=0)
            rows = [x.reshape(16, 8, N2) for x in (even[:, s], last)]
            sg_send[16 * p : 16 * (p + 1), c] = jnp.concatenate(rows, axis=1).astype(BF16)
        for z in (2, 1, 3, 0):
            for x in (2, 1, 3, 0):
                e = 16 * p + ((my_z + z) & 3) * 4 + ((my_x + x) & 3)
                if z or x:
                    remote(sg_send.at[e], sg_dst, 3, {"ctx": e})
                else:

                    @pl.when(my_y != p)
                    def _():
                        remote(sg_send.at[e], sg_dst, 3, {"ctx": e})

    local(sg_send.at[me], sg_dst, 3)

    finish(l_recv, recv_sem.at[5])
    total = jnp.sum(l_recv[...].reshape(64, 8, N2), axis=0)
    long_out[...] = total[:4] + total[4:]
    finish(s_recv, recv_sem.at[6])
    short_out[...] = jnp.sum(s_recv[...], axis=0)
    finish(sg_recv, recv_sem.at[3])
    finish(f_buf.at[pl.ds(0, n_peers)], send_sem.at[0])
    finish(send.at[pl.ds(0, n_peers)], send_sem.at[1])
    for q in range(2):
        finish(send.at[pl.ds(0, n_peers), q], send_sem.at[2 + 5 * q])
    finish(sg_send.at[pl.ds(0, n_peers)], send_sem.at[3])
    finish(l_send.at[pl.ds(0, 4 * (n_all - 1)), :], send_sem.at[5])
    finish(s_recv.at[pl.ds(0, n_all - 1)], send_sem.at[6])


def lay_out(sg_in, long_in, short_in, swap_in, sg_out, long_out, short_out, rows, sem):
    copies = [
        pltpu.make_async_copy(long_in, long_out, sem.at[2]),
        pltpu.make_async_copy(short_in, short_out, sem.at[3]),
    ]
    for c in copies:
        c.start()
    for g in range(2):
        x = jnp.concatenate(
            [sg_in[32 * g + 16 * h : 32 * g + 16 * (h + 1)].reshape(256, N2) for h in range(2)], axis=1
        )
        y = dot(swap_in[...], x).astype(BF16)
        for h in range(2):
            ch = slice(32 * g + 16 * h, 32 * g + 16 * (h + 1))
            for a in range(16):
                rows[ch, N2 * a : N2 * (a + 1)] = y[16 * a : 16 * (a + 1), h * N2 : (h + 1) * N2]
        part = pl.ds(32 * g, 32)
        copies.append(pltpu.make_async_copy(rows.at[part, :], sg_out.at[part, :], sem.at[g]))
        copies[-1].start()
    for c in copies:
        c.wait()


def shards(signal, grad_out, long_filter, short_filter, long_skip, short_skip):
    n_ctx, n_tp = lax.axis_size("ctx"), lax.axis_size("tp")
    consts = [jnp.asarray(t) for t in tables()]
    hbm = pl.BlockSpec(memory_space=pltpu.HBM)
    vmem = pl.BlockSpec(memory_space=pltpu.VMEM)
    V, S = pltpu.VMEM, pltpu.SMEM
    spec = V((N1, 2 * N2), F32)
    raw = pl.pallas_call(
        lambda *refs: kernel(n_ctx, n_tp, *refs),
        out_shape=(
            pltpu.VMEM((64, 16, N2), BF16),
            pltpu.VMEM((4, N2), F32),
            pltpu.VMEM((1, N2), F32),
            pltpu.VMEM((256, 256), BF16),
        ),
        in_specs=[hbm] * 10,
        out_specs=(vmem, vmem, vmem, vmem),
        scratch_shapes=[
            V((64, 2048), BF16), V((64, 2048), BF16), V((16, N2), F32), V((2, 8, N2), F32),
            V((1, N2), F32), S((64,), F32), S((64,), F32),
            V((2 * N1, N1), BF16), V((N1, 2 * N1), BF16), V((768, 2 * N2), F32), V((1536, 256), BF16),
            V((64, 2, 16, N2), BF16), V((2, 32, 2, 16, N2), BF16), V((32, 2, 8, N2), F32),
            spec, spec, spec, spec, spec, spec, spec, V((2, N1, N2), F32), V((HALF + 8, N2), F32),
            V((768, N2), BF16), V((384, N2), BF16), spec,
            V((N1, N2), F32), V((N1, N2), F32), V((1, N2), F32), V((128, 1, N2), F32), V((32, 2, 16, N2), BF16),
            pltpu.SemaphoreType.DMA((10,)), pltpu.SemaphoreType.DMA((8,)), pltpu.SemaphoreType.DMA((8,)),
            pltpu.SemaphoreType.REGULAR,
        ],
        compiler_params=pltpu.CompilerParams(
            collective_id=0, has_side_effects=True, vmem_limit_bytes=60 * 1024 * 1024
        ),
        cost_estimate=pl.CostEstimate(flops=6_000_000_000, bytes_accessed=8_000_000, transcendentals=0),
    )(
        signal, grad_out, long_filter.reshape(16, N2), short_filter.reshape(1, N2),
        long_skip, short_skip, *consts,
    )
    sg, long, short = pl.pallas_call(
        lay_out,
        out_shape=(
            jax.ShapeDtypeStruct((64, 2048), BF16),
            jax.ShapeDtypeStruct((4, N2), F32),
            jax.ShapeDtypeStruct((1, N2), F32),
        ),
        in_specs=[vmem, vmem, vmem, vmem],
        out_specs=(hbm, hbm, hbm),
        scratch_shapes=[V((64, 2048), BF16), pltpu.SemaphoreType.DMA((4,))],
    )(*[pltpu.with_memory_space_constraint(r, pltpu.VMEM) for r in raw])
    return sg, long.reshape(512), short.reshape(N2)


def solution(mesh):
    placed = (P("tp", "ctx"), P("tp", "ctx"), P("ctx"), P(), P("tp"), P("tp"))
    return jax.shard_map(
        shards,
        mesh=mesh,
        in_specs=placed,
        out_specs=(P("tp", "ctx"), P(("ctx", "tp")), P()),
        check_vma=False,
    )
```

```python
import math

import jax
import jax.numpy as jnp
import ml_dtypes
import numpy as np
from jax import lax
from jax.experimental import pallas as pl
from jax.experimental.pallas import tpu as pltpu
from jax.sharding import PartitionSpec as P

MESH = pl.DeviceIdType.MESH
F32, BF16 = jnp.float32, jnp.bfloat16
N1, N2 = 512, 128
LEN = N1 * N2
HALF = N1 // 2


def split_np(x):
    x = x.astype(np.float32)
    hi = x.astype(ml_dtypes.bfloat16)
    lo = (x - hi.astype(np.float32)).astype(ml_dtypes.bfloat16)
    return hi, lo


def tables():
    k = np.arange(N1, dtype=np.float64)[:, None] + 0.25
    kh = k[:HALF]
    fwd, inv = [], []
    for odd in range(2):
        n = 2 * np.arange(HALF, dtype=np.float64)[None, :] + odd
        ang = -2 * np.pi * np.mod(kh * n, N1) / N1
        hi, lo = split_np(np.concatenate([np.cos(ang), np.sin(ang)], axis=0))
        fwd.append(np.concatenate([hi, lo], axis=1))
        inv.append(np.concatenate([hi.T, lo.T], axis=1))
    m = np.arange(N2, dtype=np.float64)
    ang = -2 * np.pi * k * m[None, :] / LEN
    twist = np.concatenate([np.cos(ang), np.sin(ang)], axis=1)
    ang = np.broadcast_to(-2 * np.pi * kh / N1, (HALF, N2))
    twist = np.concatenate([twist, np.concatenate([np.cos(ang), np.sin(ang)], axis=1)]).astype(np.float32)
    ang = -2 * np.pi * np.mod(m[:, None] * m[None, :], N2) / N2
    br, bi = np.cos(ang), np.sin(ang)
    b_hi, b_lo = split_np(np.block([[br, bi], [-bi, br]]))
    c_hi, c_lo = split_np(np.block([[br, -bi], [bi, br]]) / LEN)
    mix = np.concatenate([b_hi, b_hi, b_lo, c_hi, c_hi, c_lo])
    return np.concatenate(fwd), np.concatenate(inv), twist, mix


def dot(a, b):
    return jnp.dot(a, b, preferred_element_type=F32)


def split(x):
    hi = x.astype(BF16)
    return hi, (x - hi.astype(F32)).astype(BF16)


def split3(x):
    hi, lo = split(x)
    return jnp.concatenate([hi, lo, hi], axis=1)


def twice(x):
    return jnp.concatenate([x, x], axis=0)


def mix_forward(even, odd, twist, mix, z_refs):
    for q, z in enumerate(z_refs):
        s = slice(q * N2, (q + 1) * N2)
        er, ei, dr, di = even[:HALF, s], even[HALF:, s], odd[:HALF, s], odd[HALF:, s]
        for h, (xr, xi) in enumerate([(er + dr, ei + di), (er - dr, ei - di)]):
            r = slice(h * HALF, (h + 1) * HALF)
            tr, ti = twist[r, :N2], twist[r, N2:]
            y = jnp.concatenate([xr * tr - xi * ti, xi * tr + xr * ti], axis=1)
            z[r, :] = dot(split3(y), mix[:768, :])


def forward_exact(xe, xo, fwd, twist, mix, z_refs):
    mix_forward(dot(fwd[:N1, :], twice(xe)), dot(fwd[N1:, :], twice(xo)), twist, mix, z_refs)


def forward_filter(fe, fo, fwd, twist, mix, z):
    hi, lo = split(jnp.concatenate([fe, fo], axis=1))
    yr, yi = (dot(fwd[r, :], twice(hi)) + dot(fwd[r, :HALF], lo) for r in (slice(0, HALF), slice(HALF, N1)))
    tr, ti = twist[N1:, :N2], twist[N1:, N2:]
    dr, di = yr[:, N2:], yi[:, N2:]
    even = jnp.concatenate([yr[:, :N2], yi[:, :N2]], axis=0)
    odd = jnp.concatenate([dr * tr - di * ti, di * tr + dr * ti], axis=0)
    mix_forward(even, odd, twist, mix, (z,))


def inverse_mix(a, b, twist, mix):
    ys = []
    for h in range(2):
        r = slice(h * HALF, (h + 1) * HALF)
        ar, ai, br, bi = a[r, :N2], a[r, N2:], b[r, :N2], b[r, N2:]
        z = jnp.concatenate([ar * br + ai * bi, ai * br - ar * bi], axis=1)
        y = dot(split3(z), mix[768:, :])
        yr, yi = y[:, :N2], y[:, N2:]
        tr, ti = twist[r, :N2], twist[r, N2:]
        ys.append(jnp.concatenate([yr * tr + yi * ti, yi * tr - yr * ti], axis=0))
    return ys[0] + ys[1], ys[0] - ys[1]


def inverse_rows(halves, inv):
    out = []
    for h in range(2):
        hi, lo = split(jnp.concatenate([x[h] for x in halves], axis=1))
        r = slice(h * HALF, (h + 1) * HALF)
        out.append(dot(inv[r, :], twice(hi)) + dot(inv[r, :N1], lo))
    return out


def one_hot(cond):
    return jnp.where(cond, 1.0, 0.0).astype(BF16)


def swap_matrix(back):
    i = lax.broadcasted_iota(jnp.int32, (256, 256), 0)
    j = lax.broadcasted_iota(jnp.int32, (256, 256), 1)
    if back:
        i, j = j, i
    p = i % 16
    return one_hot((i // 16 == j % 16) & (2 * (p % 8) + p // 8 == j // 16))


def rolled(w_row, first, rows):
    zero = jnp.zeros((1, N2), F32)
    base = jnp.concatenate([w_row, zero] if first else [zero, w_row], axis=1)
    return pltpu.roll(jnp.broadcast_to(base, (rows, 2 * N2)), 0, 1, stride=1, stride_axis=0)


def stack3(x):
    hi, lo = split(x)
    return jnp.concatenate([hi, hi, lo], axis=0)


def row_pairs(re, ro, r_buf):
    se, so = re[0] + re[1], ro[0] + ro[1]
    r_buf[:HALF, :] = se
    return jnp.concatenate(
        [jnp.concatenate([se, so], axis=1), jnp.concatenate([so, r_buf[pl.ds(1, HALF), :]], axis=1)], axis=0
    )


def turned_filter(fe, fo):
    i = lax.broadcasted_iota(jnp.int32, (N2, N2), 0)
    j = lax.broadcasted_iota(jnp.int32, (N2, N2), 1)
    flip = one_hot(i + j == N2 - 1)
    hi, lo = split(jnp.transpose(jnp.concatenate([fe, fo], axis=0)))
    return dot(flip, hi).astype(BF16), dot(flip, lo).astype(BF16)


def short_row(pair, f_hi, f_lo, re, lam):
    hi, lo = split(pair)
    cross = dot(f_hi, hi) + (dot(f_hi, lo) + dot(f_lo, hi))
    diag = pltpu.roll(cross, N2 + 1, 1, stride=1, stride_axis=0)
    short = jnp.sum(diag, axis=0, keepdims=True)[:, :N2]
    return short + (lam[0] * re[0][:1, :] + lam[1] * re[1][:1, :])


def filter_product(zf, zw, lam, alpha, zv):
    fr, fi = zf[:, :N2] + lam, zf[:, N2:]
    wr, wi = zw[:, :N2] + alpha, zw[:, N2:]
    zv[:, :N2] = fr * wr - fi * wi
    zv[:, N2:] = fr * wi + fi * wr


def tail_matrix(f_last, band):
    tail = dot(split3(f_last), band)
    i = lax.broadcasted_iota(jnp.int32, (N2, N2), 0)
    j = lax.broadcasted_iota(jnp.int32, (N2, N2), 1)
    flip = one_hot(i + j == N2)
    hi, lo = split(tail)
    turned = (dot(hi, flip) + dot(lo, flip))[7:, :]
    return rolled(turned, True, N2)[:, :N2]


def halves(x):
    x = x.astype(F32)
    return x[:, :8].reshape(HALF, N2).astype(BF16), x[:, 8:].reshape(HALF, N2).astype(BF16)


def offsets():
    def far(o):
        return o[0] + min(o[1], 4 - o[1]) + min(o[2], 4 - o[2])

    out = [(y, z, x) for y in range(2) for z in range(4) for x in range(4)][1:]
    return sorted(out, key=lambda o: -far(o))


def all_offsets():
    def far(o):
        y = (1 if o[1] else 2) if o[0] & 2 else o[1]
        return y + min(o[2], 4 - o[2]) + min(o[3], 4 - o[3])

    out = [(t, y, z, x) for y in range(2) for z in range(4) for x in range(4) for t in range(4)][1:]
    return sorted(out, key=lambda o: -far(o))


def kernel(
    n_ctx, n_tp,
    sig, cot, filt, w_in, lam_in, alpha_in, f_tab, i_tab, t_tab, m_tab,
    sg_recv, long_out, short_out,
    sig_v, cot_v, filt_v, filt_s, w_v, lam_s, alpha_s, fwd, inv, twist, mix,
    send, recv, f_buf, zs0, zg0, zs1, zg1, zf, zv0, zv1, half, r_buf, band_a, band_c, zw,
    l_send, l_recv, s_send, s_recv, sg_send, load_sem, send_sem, recv_sem, ready,
):
    me, tp = lax.axis_index("ctx"), lax.axis_index("tp")
    zs, zg, zv = (zs0, zs1), (zg0, zg1), (zv0, zv1)
    my_y, my_z, my_x = me // 16, (me // 4) % 4, me % 4
    at = {(y, z, x): (my_y ^ y) * 16 + ((my_z + z) & 3) * 4 + ((my_x + x) & 3) for y, z, x in [(0, 0, 0)] + offsets()}
    peers = [at[o] for o in offsets()]
    tp_peers = [tp ^ i for i in (3, 2, 1)]
    n_peers = len(peers)
    n_all = n_ctx * n_tp
    my_id = n_tp * me + tp

    barrier = pltpu.get_barrier_semaphore()
    for e in peers:
        pl.semaphore_signal(barrier, inc=1, device_id={"ctx": e}, device_id_type=MESH)
    for t in tp_peers:
        pl.semaphore_signal(barrier, inc=1, device_id={"tp": t}, device_id_type=MESH)
    loads = [
        pltpu.make_async_copy(src, dst, load_sem.at[i])
        for i, (src, dst) in enumerate(
            [(filt, filt_v), (sig, sig_v), (cot, cot_v), (w_in, w_v), (lam_in, lam_s), (alpha_in, alpha_s),
             (f_tab, fwd), (t_tab, twist), (m_tab, mix), (i_tab, inv)]
        )
    ]
    for c in loads:
        c.start()
    r_buf[HALF:, :] = jnp.zeros((8, N2), F32)
    swap = swap_matrix(False)
    for c in loads[:6]:
        c.wait()
    for h in range(2):
        for i in range(8):
            filt_s[h, i : i + 1, :] = filt_v[2 * i + h : 2 * i + h + 1, :]
    for g in range(4):
        ch = slice(16 * g, 16 * (g + 1))
        x = jnp.concatenate(
            [
                jnp.concatenate([v[ch, N2 * a : N2 * (a + 1)] for a in range(16)], axis=0)
                for v in (sig_v, cot_v)
            ],
            axis=1,
        )
        y = dot(swap, x).astype(BF16)
        send[ch, 0] = y[:, :N2].reshape(16, 16, N2)
        send[ch, 1] = y[:, N2:].reshape(16, 16, N2)
    pl.semaphore_wait(barrier, n_peers + len(tp_peers))
    for t in tp_peers:
        pl.semaphore_signal(ready, inc=1, device_id={"tp": t}, device_id_type=MESH)

    f_dst = f_buf.at[me]

    def remote(src, dst, k, where):
        pltpu.make_async_remote_copy(
            src_ref=src, dst_ref=dst, send_sem=send_sem.at[k], recv_sem=recv_sem.at[k],
            device_id=where, device_id_type=MESH,
        ).start()

    def local(src, dst, k):
        pltpu.make_async_copy(src, dst, recv_sem.at[k]).start()

    def finish(ref, sem):
        pltpu.make_async_copy(ref, ref, sem).wait()

    for c in range(2):
        for e in peers:
            remote(send.at[2 * e + c], recv.at[c, me], 1 + c, {"ctx": e})
    for e in peers:
        remote(filt_s, f_dst, 0, {"ctx": e})
    for c in range(2):
        local(send.at[2 * me + c], recv.at[c, me], 1 + c)
    local(filt_s, f_dst, 0)

    w_row = w_v[...]
    band_a[...] = stack3(jnp.transpose(rolled(w_row, True, N2)))
    band_c[...] = stack3(rolled(w_row, False, N2)[:, :N2])
    alpha = (alpha_s[2 * me], alpha_s[2 * me + 1])
    lam = (lam_s[2 * me], lam_s[2 * me + 1])
    for c in loads[6:]:
        c.wait()
    zw[...] = dot(split3(twist[:N1, :] * jnp.concatenate([w_row, w_row], axis=1)), mix[:768, :])

    for c in range(2):
        finish(recv.at[c], recv_sem.at[1 + c])
        se, so = halves(recv[c, :, 0])
        ge, go = halves(recv[c, :, 1])
        forward_exact(
            jnp.concatenate([se, ge], axis=1), jnp.concatenate([so, go], axis=1), fwd, twist, mix, (zs[c], zg[c])
        )
        part = inverse_mix(zg[c], zs[c], twist, mix)
        if c == 0:
            half[0], half[1] = part
    even, odd = inverse_rows([(half[0], half[1]), part], inv)
    re, ro = (even[:, :N2], even[:, N2:]), (odd[:, :N2], odd[:, N2:])
    pair = row_pairs(re, ro, r_buf)
    pl.semaphore_wait(ready, len(tp_peers))
    everyone = [(at[o[1:]], tp ^ o[0]) for o in all_offsets()]
    l_dst = l_recv.at[pl.ds(pl.multiple_of(4 * my_id, 4), 4), :]
    steps = sorted(
        [(t, z, x) for t in range(4) for z in range(4) for x in range(4)],
        key=lambda o: -((o[0] & 2) + min(o[1], 4 - o[1]) + min(o[2], 4 - o[2])),
    )
    for p in range(2):
        m = slice(128 * p, 128 * (p + 1))
        m2 = slice(HALF + 128 * p, HALF + 128 * (p + 1))
        rows = dot(split3(jnp.concatenate([pair[m], pair[m2]], axis=0)), band_a[...])
        l_send[pl.ds(HALF * p, 128, 2), :] = rows[:128] + (alpha[0] * re[0][m] + alpha[1] * re[1][m])
        l_send[pl.ds(HALF * p + 1, 128, 2), :] = rows[128:] + (alpha[0] * ro[0][m] + alpha[1] * ro[1][m])
        for t, z, x in steps:
            e = 16 * p + ((my_z + z) & 3) * 4 + ((my_x + x) & 3)
            src = l_send.at[pl.ds(pl.multiple_of(4 * (n_tp * e + (tp ^ t)), 4), 4), :]
            if t or z or x:
                remote(src, l_dst, 5, {"ctx": e, "tp": tp ^ t})
            else:

                @pl.when(my_y != p)
                def _():
                    remote(src, l_dst, 5, {"ctx": e, "tp": tp ^ t})

    local(l_send.at[pl.ds(pl.multiple_of(4 * my_id, 4), 4), :], l_dst, 5)

    finish(f_buf, recv_sem.at[0])
    fe, fo = f_buf[:, 0].reshape(HALF, N2), f_buf[:, 1].reshape(HALF, N2)
    ft_hi, ft_lo = turned_filter(fe, fo)
    s_send[...] = short_row(pair, ft_hi, ft_lo, re, lam)
    for e, t in everyone:
        remote(s_send, s_recv.at[my_id], 6, {"ctx": e, "tp": t})
    local(s_send, s_recv.at[my_id], 6)
    forward_filter(fe, fo, fwd, twist, mix, zf)
    t_hi, t_lo = split(tail_matrix(fo[HALF - 8 :, :], band_c[...]))
    for c in range(2):
        filter_product(zf, zw, lam[c], alpha[c], zv[c])
    halves_sg = [inverse_mix(zg[c], zv[c], twist, mix) for c in range(2)]
    sg_dst = sg_recv.at[pl.ds(2 * me, 2)]
    folds = [(dot(recv[c, 0, 1], t_hi) + dot(recv[c, 0, 1], t_lo))[:1, :] for c in range(2)]
    ys = [split(jnp.concatenate([x[h] for x in halves_sg], axis=1)) for h in range(2)]
    for p in range(2):
        even, odd = (
            dot(inv[r, :], twice(hi)) + dot(inv[r, :N1], lo)
            for (hi, lo), r in zip(ys, (slice(h * HALF + 128 * p, h * HALF + 128 * (p + 1)) for h in range(2)))
        )
        for c in range(2):
            s = slice(c * N2, (c + 1) * N2)
            last = odd[:, s]
            if p == 1:
                last = jnp.concatenate([last[:127], last[127:] + folds[c]], axis=0)
            rows = [x.reshape(16, 8, N2) for x in (even[:, s], last)]
            sg_send[16 * p : 16 * (p + 1), c] = jnp.concatenate(rows, axis=1).astype(BF16)
        for z in (2, 1, 3, 0):
            for x in (2, 1, 3, 0):
                e = 16 * p + ((my_z + z) & 3) * 4 + ((my_x + x) & 3)
                if z or x:
                    remote(sg_send.at[e], sg_dst, 3, {"ctx": e})
                else:

                    @pl.when(my_y != p)
                    def _():
                        remote(sg_send.at[e], sg_dst, 3, {"ctx": e})

    local(sg_send.at[me], sg_dst, 3)

    finish(l_recv, recv_sem.at[5])
    total = jnp.sum(l_recv[...].reshape(64, 8, N2), axis=0)
    long_out[...] = total[:4] + total[4:]
    finish(s_recv, recv_sem.at[6])
    short_out[...] = jnp.sum(s_recv[...], axis=0)
    finish(sg_recv, recv_sem.at[3])
    finish(f_buf.at[pl.ds(0, n_peers)], send_sem.at[0])
    for c in range(2):
        finish(send.at[pl.ds(0, n_peers)], send_sem.at[1 + c])
    finish(sg_send.at[pl.ds(0, n_peers)], send_sem.at[3])
    finish(l_send.at[pl.ds(0, 4 * (n_all - 1)), :], send_sem.at[5])
    finish(s_recv.at[pl.ds(0, n_all - 1)], send_sem.at[6])


def lay_out(sg_in, long_in, short_in, sg_out, long_out, short_out, rows, sem):
    swap = swap_matrix(True)
    copies = [
        pltpu.make_async_copy(long_in, long_out, sem.at[2]),
        pltpu.make_async_copy(short_in, short_out, sem.at[3]),
    ]
    for c in copies:
        c.start()
    for g in range(2):
        x = jnp.concatenate(
            [sg_in[32 * g + 16 * h : 32 * g + 16 * (h + 1)].reshape(256, N2) for h in range(2)], axis=1
        )
        y = dot(swap, x).astype(BF16)
        for h in range(2):
            ch = slice(32 * g + 16 * h, 32 * g + 16 * (h + 1))
            for a in range(16):
                rows[ch, N2 * a : N2 * (a + 1)] = y[16 * a : 16 * (a + 1), h * N2 : (h + 1) * N2]
        part = pl.ds(32 * g, 32)
        copies.append(pltpu.make_async_copy(rows.at[part, :], sg_out.at[part, :], sem.at[g]))
        copies[-1].start()
    for c in copies:
        c.wait()


def shards(signal, grad_out, long_filter, short_filter, long_skip, short_skip):
    n_ctx, n_tp = lax.axis_size("ctx"), lax.axis_size("tp")
    consts = [jnp.asarray(t) for t in tables()]
    hbm = pl.BlockSpec(memory_space=pltpu.HBM)
    vmem = pl.BlockSpec(memory_space=pltpu.VMEM)
    V, S = pltpu.VMEM, pltpu.SMEM
    spec = V((N1, 2 * N2), F32)
    raw = pl.pallas_call(
        lambda *refs: kernel(n_ctx, n_tp, *refs),
        out_shape=(
            pltpu.VMEM((64, 16, N2), BF16),
            pltpu.VMEM((4, N2), F32),
            pltpu.VMEM((1, N2), F32),
        ),
        in_specs=[hbm] * 10,
        out_specs=(vmem, vmem, vmem),
        scratch_shapes=[
            V((64, 2048), BF16), V((64, 2048), BF16), V((16, N2), F32), V((2, 8, N2), F32),
            V((1, N2), F32), S((64,), F32), S((64,), F32),
            V((2 * N1, N1), BF16), V((N1, 2 * N1), BF16), V((768, 2 * N2), F32), V((1536, 256), BF16),
            V((64, 2, 16, N2), BF16), V((2, 32, 2, 16, N2), BF16), V((32, 2, 8, N2), F32),
            spec, spec, spec, spec, spec, spec, spec, V((2, N1, N2), F32), V((HALF + 8, N2), F32),
            V((768, N2), BF16), V((384, N2), BF16), spec,
            V((N1, N2), F32), V((N1, N2), F32), V((1, N2), F32), V((128, 1, N2), F32), V((32, 2, 16, N2), BF16),
            pltpu.SemaphoreType.DMA((10,)), pltpu.SemaphoreType.DMA((7,)), pltpu.SemaphoreType.DMA((7,)),
            pltpu.SemaphoreType.REGULAR,
        ],
        compiler_params=pltpu.CompilerParams(
            collective_id=0, has_side_effects=True, vmem_limit_bytes=60 * 1024 * 1024
        ),
        cost_estimate=pl.CostEstimate(flops=6_000_000_000, bytes_accessed=8_000_000, transcendentals=0),
    )(
        signal, grad_out, long_filter.reshape(16, N2), short_filter.reshape(1, N2),
        long_skip, short_skip, *consts,
    )
    sg, long, short = pl.pallas_call(
        lay_out,
        out_shape=(
            jax.ShapeDtypeStruct((64, 2048), BF16),
            jax.ShapeDtypeStruct((4, N2), F32),
            jax.ShapeDtypeStruct((1, N2), F32),
        ),
        in_specs=[vmem, vmem, vmem],
        out_specs=(hbm, hbm, hbm),
        scratch_shapes=[V((64, 2048), BF16), pltpu.SemaphoreType.DMA((4,))],
    )(*[pltpu.with_memory_space_constraint(r, pltpu.VMEM) for r in raw])
    return sg, long.reshape(512), short.reshape(N2)


def solution(mesh):
    placed = (P("tp", "ctx"), P("tp", "ctx"), P("ctx"), P(), P("tp"), P("tp"))
    return jax.shard_map(
        shards,
        mesh=mesh,
        in_specs=placed,
        out_specs=(P("tp", "ctx"), P(("ctx", "tp")), P()),
        check_vma=False,
    )
```
